256 devices in a mesh: row: 32 (over z, x), col: 8 (over y, core).
Axes of the slice: x: 4, y: 4, z: 8, core: 2. Of those that a mesh axis runs over, the one named last changes fastest.
Arguments:
- eigvecs: float32 [98304, 2048], P('row', 'col'), may hold values from -6 to 6
- reflectors: float32 [98304, 2048], P('row', 'col'), may hold values from -0.21875 to 0.21875
- factors: float32 [8, 256, 256], P('col'), may hold values from -3 to 3, as said below
Outputs:
- transformed: float32 [98304, 2048], P('row', 'col')
The draws below stay inside these ranges and needn't reach their ends.
Inputs may be any that keep to these rules, and one draw needn't show every extreme that they name: Each slab of factors is upper triangular with its diagonal between 0.5 and 2.
All inputs are finite; a program needn't handle non-finite values.
Results may differ from the reference program's by a relative error of at most 0.00017.
Values sent between devices are 32-bit elements; how exact they have to be, the bound alone decides.
A program may use at most 64 MiB of HBM per device.

```python
import math
import jax
import jax.numpy as jnp
from jax import lax

NB = 256
ORDER = 98304
EIGS = 2048
PANEL_COLS = 2048
N_COL = 8


def draw_factors(key, part):
    key = jax.random.fold_in(key, 7)
    key_upper, key_diag = jax.random.split(key)
    upper = jax.random.normal(key_upper, (N_COL, NB, NB), jnp.float32) / math.sqrt(NB)
    diag_vals = jax.random.uniform(key_diag, (N_COL, NB, 1), jnp.float32, 0.5, 2.0)
    rows_idx = lax.broadcasted_iota(jnp.int32, (1, NB, NB), 1)
    cols_idx = lax.broadcasted_iota(jnp.int32, (1, NB, NB), 2)
    filled = jnp.where(cols_idx > rows_idx, upper, jnp.where(cols_idx == rows_idx, diag_vals, 0.0))
    return jnp.clip(filled, -3.0, 3.0)


def block_levels(key, shape, shards, least, largest):
    loudness, own = 1.0, jax.random.fold_in(key, 6)
    for dim, blocks in shards:
        steps = jnp.exp(jax.random.uniform(jax.random.fold_in(own, dim), (blocks,), jnp.float32, least / len(shards), largest / len(shards)))
        loudness = loudness * jnp.repeat(steps, shape[dim] // blocks).reshape([-1 if axis == dim else 1 for axis in range(len(shape))])
    return loudness


def bell_draw(rng, dims, deviation, bound, cuts=(), kind=jnp.bfloat16):
    level = block_levels(rng, dims, cuts, -0.22, 0.18) if cuts else 1.0
    entries = jax.random.normal(rng, dims, jnp.float32) * deviation * level
    return jnp.minimum(jnp.maximum(entries, -bound), bound).astype(kind)


def setup_inputs(seed: int = 0) -> dict:
    keys = jax.random.split(jax.random.key(seed), 4)
    eigvecs = bell_draw(keys[0], (ORDER, EIGS), 1.0, 6.0, ((0, 32), (1, 8)), jnp.float32)
    reflectors = bell_draw(keys[1], (ORDER, PANEL_COLS), ((ORDER * NB) ** -0.25), 0.21875, ((0, 32), (1, 8)), jnp.float32)
    factors = draw_factors(jax.random.fold_in(keys[3], 71), 0)
    return dict(eigvecs=eigvecs, reflectors=reflectors, factors=factors)


def matmul(left, right):
    return jnp.dot(left, right, precision=lax.Precision.HIGHEST, preferred_element_type=jnp.float32)


def apply_panel(field, vectors, factor):
    projected = matmul(vectors.T, field)
    return field - matmul(vectors, matmul(factor, projected))


def reference(eigvecs, reflectors, factors):
    first_v = reflectors[:, NB:2 * NB]
    second_v = reflectors[:, :NB]
    middle = apply_panel(eigvecs, first_v, factors[1])
    return apply_panel(middle, second_v, factors[0])
```

```python
import jax
import jax.numpy as jnp
from jax import lax
from jax.experimental import pallas as pl
from jax.experimental.pallas import tpu as pltpu
from jax.sharding import PartitionSpec as P

MESH = pl.DeviceIdType.MESH
F32, BF16 = jnp.float32, jnp.bfloat16
NZ, NX, NCOL = 8, 4, 8
NB = 256
ROWS = 3072
HALF = ROWS // 2
TICK = 16
GROUP = 64
TICKS = GROUP // TICK
PER_PANEL = NB // GROUP
GROUPS = 2 * PER_PANEL
CHUNKS = GROUPS * TICKS
TILE = 128


def split(value):
    high = value.astype(BF16)
    return high, (value - high.astype(F32)).astype(BF16)


def dot(left, right):
    return jnp.dot(left, right, preferred_element_type=F32)


def dot_nt(left, right):
    return lax.dot_general(left, right, (((1,), (1,)), ((), ())), preferred_element_type=F32)


def product(left, right):
    lh, ll = split(left)
    rh, rl = split(right)
    return dot(lh, rh) + dot(lh, rl) + dot(ll, rh)


def kernel(
    e_hbm, v_hbm, f_hbm, out_hbm,
    e, raw, eh, el, vt, vn,
    wloc, rs_land, xs, x_land, red, ag_land, wfull,
    ms, mz_land, mz, mx_land, mats,
    gacc, gloc, gz_land, gq, gx_land,
    s_stack, s_low,
    load_sem, out_sem, recv, send, sib,
    rs_s, rs_r, x_s, x_r, ag_s, ag_r,
    ms_s, ms_r, mz_s, mz_r, mx_s, mx_r,
    gz_s, gz_r, gx_s, gx_r,
):
    row = lax.axis_index("row")
    col = lax.axis_index("col")
    z, x = row // NX, row % NX
    y, core = col // 2, col % 2

    def ring(yy, cc):
        return (row, yy * 2 + cc)

    def z_peer(d):
        return (lax.rem(z + d, NZ) * NX + x, col)

    def x_peer(d):
        return (z * NX + lax.rem(x + d, NX), col)

    at_root = y == 0
    first = ((core == 1) & (y == 1)) | ((core == 0) & (y == 3))
    last = ((core == 1) & (y == 3)) | ((core == 0) & (y == 1))
    ahead = jnp.where(core == 1, y + 1, y - 1)
    behind = jnp.where(core == 1, y - 1, y + 1)
    lag = jnp.where(first, 2, 1)
    mine = 1 - core
    rank = x * NZ + z

    def remote(src, dst, send_sem, recv_sem, device):
        return pltpu.make_async_remote_copy(
            src_ref=src, dst_ref=dst, send_sem=send_sem, recv_sem=recv_sem, device_id=device, device_id_type=MESH
        )

    load_e = pltpu.make_async_copy(e_hbm, e, load_sem.at[0])
    load_v = pltpu.make_async_copy(v_hbm, raw, load_sem.at[1])
    load_f = pltpu.make_async_copy(
        f_hbm.at[0, pl.ds(pl.multiple_of(rank * 8, 8), 8), :], ms.at[1 - core], load_sem.at[2]
    )

    @pl.when(at_root)
    def _():
        load_v.start()
        load_f.start()

    load_e.start()

    barrier = pltpu.get_barrier_semaphore()

    def greet(device):
        pl.semaphore_signal(barrier, inc=1, device_id=device, device_id_type=MESH)

    for d in range(1, NZ):
        greet(z_peer(d))
    for d in range(1, NX):
        greet(x_peer(d))
    greet(ring(y, 1 - core))

    @pl.when(jnp.logical_not(at_root))
    def _():
        greet(ring(0, 0))
        greet(ring(0, 1))

    @pl.when(jnp.logical_not(at_root | first))
    def _():
        greet(ring(behind, core))

    def transpose_in(ct):
        panel = 1 - core

        def body(rt, _):
            start = pl.multiple_of(rt * TILE, TILE)
            for h in range(2):
                block = raw[pl.ds(pl.multiple_of(h * HALF + start, TILE), TILE), ct * TILE : (ct + 1) * TILE]
                vt[panel, h, ct * TILE : (ct + 1) * TILE, pl.ds(start, TILE)] = block.T
            return 0

        lax.fori_loop(0, HALF // TILE, body, 0)

    @pl.when(at_root)
    def _():
        load_v.wait()
        load_f.wait()
        transpose_in(0)

    pl.semaphore_wait(barrier, (NZ - 1) + (NX - 1) + jnp.where(at_root, 7, jnp.where(last, 1, 2)))

    def spread(m):
        for d in range(1, NCOL):
            yield remote(ms.at[m], ms.at[m], ms_s.at[m], ms_r.at[m], (row, lax.rem(col + d, NCOL)))

    for m in range(2):

        @pl.when(at_root & (core == 1 - m))
        def _():
            for copy in spread(m):
                copy.start()

    def row0(g):
        return pl.multiple_of(jnp.where(g < PER_PANEL, g, GROUPS - 1 - g) * GROUP, GROUP)

    def chunk(k, h):
        g = k // TICKS
        start = pl.multiple_of(row0(g) + (k % TICKS) * TICK, TICK)
        return vt.at[g // PER_PANEL, h, pl.ds(start, TICK), :]

    def piece(k, h, send_sem, device):
        ref = chunk(k, h)
        return remote(ref, ref, send_sem, recv.at[h, k], device)

    def ring_send(k, h):
        return piece(k, h, send.at[h, k], ring(jnp.where(h == 0, 1, 3), jnp.where(h == 0, 1, 0)))

    def sib_send(k, h):
        return piece(k, h, sib.at[h, k], ring(y, 1 - core))

    def ahead_send(k):
        return piece(k, mine, send.at[0, k], ring(ahead, core))

    def pass_on(k):
        return piece(k, mine, sib.at[0, k], ring(y, 1 - core))

    def arrived(k, h):
        piece(k, h, send.at[0, k], ring(y, 1 - core)).wait_recv()

    def ticks(i, begin, end):
        owner = at_root & ((core == 1) == (i < PER_PANEL))
        follower = at_root & ((core == 0) == (i < PER_PANEL))

        for t in range(begin, end):
            k = i * TICKS + t

            @pl.when(owner)
            def _():
                @pl.when(i % PER_PANEL != 0)
                def _():
                    for h in range(2):
                        ring_send(k - TICKS, h).wait_send()

                for h in range(2):
                    ring_send(k, h).start()
                for h in range(2):
                    sib_send(k, h).start()

            @pl.when(follower)
            def _():
                arrived(k, 0)
                arrived(k, 1)

            @pl.when(jnp.logical_not(at_root))
            def _():
                arrived(k, mine)

                @pl.when(jnp.logical_not(last))
                def _():
                    ahead_send(k).start()

                pass_on(k).start()

    def to_z(g):
        for d in range(1, NZ):
            to = lax.rem(z + d, NZ)
            yield remote(
                wloc.at[g, pl.ds(pl.multiple_of(to * 8, 8), 8), :],
                rs_land.at[g, d - 1], rs_s.at[g], rs_r.at[g], z_peer(d),
            )

    def to_x(g):
        for d in range(1, NX):
            yield remote(xs.at[g], x_land.at[g, d - 1], x_s.at[g], x_r.at[g], x_peer(d))

    def back_z(g):
        for d in range(1, NZ):
            yield remote(red.at[g], ag_land.at[g, d - 1], ag_s.at[g], ag_r.at[g], z_peer(d))

    def whole(ref, send_sem, recv_sem):
        return remote(ref, ref, send_sem, recv_sem, ring(y, 1 - core))

    def project(g):
        total = jnp.zeros((GROUP, NB), F32)
        for h in range(2):
            high, low = split(vt[g // PER_PANEL, h, pl.ds(row0(g), GROUP), :])
            both = dot(jnp.concatenate([high, low], axis=0), eh[h * HALF : (h + 1) * HALF, :])
            total += both[:GROUP] + both[GROUP:] + dot(high, el[h * HALF : (h + 1) * HALF, :])
        wloc[g] = total
        for copy in to_z(g):
            copy.start()

    def sum_z(g):
        whole(rs_land.at[g], rs_s.at[g], rs_r.at[g]).wait_recv()
        total = wloc[g, pl.ds(pl.multiple_of(z * 8, 8), 8), :]
        for d in range(NZ - 1):
            total += rs_land[g, d]
        xs[g] = total
        for copy in to_x(g):
            copy.start()

    def sum_x(g):
        whole(x_land.at[g], x_s.at[g], x_r.at[g]).wait_recv()
        total = xs[g]
        for d in range(NX - 1):
            total += x_land[g, d]
        red[g] = total
        for copy in back_z(g):
            copy.start()

    def gather(g):
        whole(ag_land.at[g], ag_s.at[g], ag_r.at[g]).wait_recv()
        base = (g // PER_PANEL) * NB + row0(jnp.int32(g))
        wfull[pl.ds(pl.multiple_of(base + z * 8, 8), 8), :] = red[g]
        for d in range(1, NZ):
            origin = lax.rem(z + NZ - d, NZ)
            wfull[pl.ds(pl.multiple_of(base + origin * 8, 8), 8), :] = ag_land[g, d - 1]

    def tile_column(j):
        return pl.multiple_of(jnp.where((j == 1) | (j == 2), TILE, 0), TILE)

    def transpose_out(j, h):
        def body(rt, _):
            start = pl.multiple_of(rt * TILE, TILE)
            block = vt[j // 2, h, pl.ds(tile_column(j), TILE), pl.ds(start, TILE)]
            high, low = split(block.T)
            rows = pl.ds(pl.multiple_of(h * HALF + start, TILE), TILE)
            vn[j, rows, :TILE] = high
            vn[j, rows, TILE:] = low
            return 0

        lax.fori_loop(0, HALF // TILE, body, 0)

    def m_to_z(m):
        for d in range(1, NZ):
            yield remote(ms.at[m], mz_land.at[m, d - 1], mz_s.at[m], mz_r.at[m], z_peer(d))

    def m_to_x(m):
        for d in range(1, NX):
            yield remote(mz.at[m], mx_land.at[m, d - 1], mx_s.at[m], mx_r.at[m], x_peer(d))

    def m_begin(m):
        is_source = at_root & ((core == 1) if m == 0 else (core == 0))

        @pl.when(jnp.logical_not(is_source))
        def _():
            whole(ms.at[m], ms_s.at[m], ms_r.at[m]).wait_recv()

        for copy in m_to_z(m):
            copy.start()

    def m_middle(m):
        whole(mz_land.at[m], mz_s.at[m], mz_r.at[m]).wait_recv()
        mz[m, pl.ds(pl.multiple_of(z * 8, 8), 8), :] = ms[m]
        for d in range(1, NZ):
            origin = lax.rem(z + NZ - d, NZ)
            mz[m, pl.ds(pl.multiple_of(origin * 8, 8), 8), :] = mz_land[m, d - 1]
        for copy in m_to_x(m):
            copy.start()

    def m_end(m):
        whole(mx_land.at[m], mx_s.at[m], mx_r.at[m]).wait_recv()
        mats[m, pl.ds(pl.multiple_of(x * 64, 64), 64), :] = mz[m]
        for d in range(1, NX):
            origin = lax.rem(x + NX - d, NX)
            mats[m, pl.ds(pl.multiple_of(origin * 64, 64), 64), :] = mx_land[m, d - 1]

    overlap_here = at_root & (core == 0)

    def overlap_to_z():
        for d in range(1, NZ):
            yield remote(gloc.at[lax.rem(z + d, NZ)], gz_land.at[d - 1], gz_s.at[0], gz_r.at[0], z_peer(d))

    def overlap_to_x():
        for d in range(1, NX):
            yield remote(gq.at[lax.rem(x + d, NX)], gx_land.at[d - 1], gx_s.at[0], gx_r.at[0], x_peer(d))

    def overlap_begin():
        gacc[...] = jnp.zeros_like(gacc)

        def body(n, _):
            h, part = n // 3, n % 3
            lanes = pl.ds(pl.multiple_of(part * 512, 512), 512)
            ah, al = split(vt[1, h, :, lanes])
            bh, bl = split(vt[0, h, :, lanes])
            gacc[...] += dot_nt(ah, bh) + dot_nt(ah, bl) + dot_nt(al, bh)
            return 0

        lax.fori_loop(0, 6, body, 0)
        for zz in range(NZ):
            for xx in range(NX):
                gloc[zz, xx] = gacc[xx * 64 + zz * 8 : xx * 64 + zz * 8 + 8, :]
        for copy in overlap_to_z():
            copy.start()

    def overlap_middle():
        whole(gz_land, gz_s.at[0], gz_r.at[0]).wait_recv()
        total = gloc[z]
        for d in range(NZ - 1):
            total += gz_land[d]
        gq[...] = total
        for copy in overlap_to_x():
            copy.start()

    def overlap_end():
        whole(gx_land, gx_s.at[0], gx_r.at[0]).wait_recv()
        total = gq[x]
        for d in range(NX - 1):
            total += gx_land[d]
        ms[2] = total
        for copy in spread(2):
            copy.start()

    def split_field():
        load_e.wait()

        def body(n, _):
            rows = pl.ds(pl.multiple_of(n * 256, 256), 256)
            high, low = split(e[rows, :])
            eh[rows, :] = high
            el[rows, :] = low
            return 0

        lax.fori_loop(0, ROWS // 256, body, 0)

    def when(condition, action, *args):
        pl.when(condition)(lambda: action(*args))

    def step(i, _):
        done = i - lag
        when(i < GROUPS, ticks, i, 0, 2)

        @pl.when(i == 0)
        def _():
            split_field()
            when(at_root, transpose_in, 1)

        when(done >= 0, project, done)
        when(i < GROUPS, ticks, i, 2, TICKS)
        when(done >= 1, lambda: transpose_out((done - 1) // 2, (done - 1) % 2))
        when(done >= 2, sum_z, done - 2)
        when(done >= 4, sum_x, done - 4)

        @pl.when(done == 1)
        def _():
            m_begin(0)
            m_begin(1)

        @pl.when(done == 3)
        def _():
            m_middle(0)
            m_middle(1)

        when(overlap_here & (i == 4), overlap_begin)
        when(overlap_here & (i == 6), overlap_middle)
        when(overlap_here & (i == 7), overlap_end)
        return 0

    def step_with_sibling(i, carry):
        done = i - lag

        @pl.when((done >= 0) & jnp.logical_not(at_root))
        def _():
            for t in range(TICKS):
                arrived(done * TICKS + t, core)

        return step(i, carry)

    lax.fori_loop(0, GROUPS + lag, step_with_sibling, 0)

    def set_s(j, value):
        high, low = split(value)
        s_stack[j, :TILE] = high
        s_stack[j, TILE:] = high
        s_low[j] = low

    def update(tiles, finish):
        def body(n, _):
            rows = pl.ds(pl.multiple_of(n * 512, 512), 512)
            total = e[rows, :]
            for j in tiles:
                part = vn[j, rows, :]
                total -= dot(part, s_stack[j]) + dot(part[:, :TILE], s_low[j])
            e[rows, :] = total
            if finish:
                pltpu.make_async_copy(e.at[rows], out_hbm.at[rows], out_sem.at[n]).start()
            return 0

        lax.fori_loop(0, ROWS // 512, body, 0)

    m_begin(2)
    sum_z(6)
    sum_x(4)
    m_end(0)
    m_end(1)
    transpose_out(3, 1)
    sum_z(7)
    sum_x(5)
    sum_x(6)
    m_middle(2)
    for g in range(4):
        gather(g)
    first_s = product(mats[0], wfull[:NB, :])
    set_s(0, first_s[:TILE])
    set_s(1, first_s[TILE:])
    sum_x(7)
    update((0, 1), False)
    m_end(2)
    gather(4)
    gather(5)
    correction = product(mats[2], first_s)
    upper = wfull[NB + TILE :, :] - correction[TILE:]
    set_s(2, product(mats[1, TILE:, TILE:], upper))
    update((2,), False)
    gather(6)
    gather(7)
    lower = wfull[NB : NB + TILE, :] - correction[:TILE]
    set_s(3, product(mats[1, :TILE, :], jnp.concatenate([lower, upper], axis=0)))
    update((3,), True)

    for g in range(GROUPS):
        whole(rs_land.at[g], rs_s.at[g], rs_r.at[g]).wait_send()
        whole(x_land.at[g], x_s.at[g], x_r.at[g]).wait_send()
        whole(ag_land.at[g], ag_s.at[g], ag_r.at[g]).wait_send()
    for m in range(3):
        whole(mz_land.at[m], mz_s.at[m], mz_r.at[m]).wait_send()
        whole(mx_land.at[m], mx_s.at[m], mx_r.at[m]).wait_send()

        @pl.when(at_root & ((core == 1) if m == 0 else (core == 0)))
        def _():
            whole(mz_land.at[m], ms_s.at[m], ms_r.at[m]).wait_send()

    @pl.when(overlap_here)
    def _():
        whole(gz_land, gz_s.at[0], gz_r.at[0]).wait_send()
        whole(gx_land, gx_s.at[0], gx_r.at[0]).wait_send()

    def drain(k, _):
        @pl.when(jnp.logical_not(at_root))
        def _():
            @pl.when(jnp.logical_not(last))
            def _():
                ahead_send(k).wait_send()

            pass_on(k).wait_send()

        @pl.when(at_root & ((core == 1) == (k < CHUNKS // 2)))
        def _():
            for h in range(2):
                sib_send(k, h).wait_send()

                @pl.when(k % (CHUNKS // 2) >= CHUNKS // 2 - TICKS)
                def _():
                    ring_send(k, h).wait_send()

        return 0

    lax.fori_loop(0, CHUNKS, drain, 0)

    def finish(n, _):
        rows = pl.ds(pl.multiple_of(n * 512, 512), 512)
        pltpu.make_async_copy(e.at[rows], out_hbm.at[rows], out_sem.at[n]).wait()
        return 0

    lax.fori_loop(0, ROWS // 512, finish, 0)


def local(eigvecs, reflectors, factors):
    vmem, dma = pltpu.VMEM, pltpu.SemaphoreType.DMA
    anywhere = pl.BlockSpec(memory_space=pl.ANY)
    return pl.pallas_call(
        kernel,
        out_shape=jax.ShapeDtypeStruct((ROWS, NB), F32),
        in_specs=[anywhere] * 3,
        out_specs=anywhere,
        scratch_shapes=[
            vmem((ROWS, NB), F32),
            vmem((ROWS, NB), F32),
            vmem((ROWS, NB), BF16),
            vmem((ROWS, NB), BF16),
            vmem((2, 2, NB, HALF), F32),
            vmem((4, ROWS, NB), BF16),
            vmem((GROUPS, GROUP, NB), F32),
            vmem((GROUPS, NZ - 1, 8, NB), F32),
            vmem((GROUPS, 8, NB), F32),
            vmem((GROUPS, NX - 1, 8, NB), F32),
            vmem((GROUPS, 8, NB), F32),
            vmem((GROUPS, NZ - 1, 8, NB), F32),
            vmem((2 * NB, NB), F32),
            vmem((3, 8, NB), F32),
            vmem((3, NZ - 1, 8, NB), F32),
            vmem((3, 64, NB), F32),
            vmem((3, NX - 1, 64, NB), F32),
            vmem((3, NB, NB), F32),
            vmem((NB, NB), F32),
            vmem((NZ, NX, 8, NB), F32),
            vmem((NZ - 1, NX, 8, NB), F32),
            vmem((NX, 8, NB), F32),
            vmem((NX - 1, 8, NB), F32),
            vmem((4, NB, NB), BF16),
            vmem((4, TILE, NB), BF16),
            dma((3,)),
            dma((ROWS // 512,)),
            dma((2, CHUNKS)),
            dma((2, CHUNKS)),
            dma((2, CHUNKS)),
            *[dma((GROUPS,))] * 6,
            *[dma((3,))] * 6,
            *[dma((1,))] * 4,
        ],
        compiler_params=pltpu.CompilerParams(collective_id=0, has_side_effects=True, vmem_limit_bytes=50 * 2**20),
    )(eigvecs, reflectors, factors)


def solution(mesh):
    in_specs = (P("row", "col"), P("row", "col"), P("col", None, None))
    return jax.shard_map(local, mesh=mesh, in_specs=in_specs, out_specs=P("row", "col"), check_vma=False)
```

```python
import jax
import jax.numpy as jnp
from jax import lax
from jax.experimental import pallas as pl
from jax.experimental.pallas import tpu as pltpu
from jax.sharding import PartitionSpec as P

MESH = pl.DeviceIdType.MESH
F32, BF16 = jnp.float32, jnp.bfloat16
NZ, NX, NCOL = 8, 4, 8
NB = 256
ROWS = 3072
HALF = ROWS // 2
TICK = 16
GROUP = 64
TICKS = GROUP // TICK
PER_PANEL = NB // GROUP
GROUPS = 2 * PER_PANEL
CHUNKS = GROUPS * TICKS
TILE = 128
DEPTH = 3
DIRECT = CHUNKS - 2
UNITS = GROUPS + 1


def split(value):
    high = value.astype(BF16)
    return high, (value - high.astype(F32)).astype(BF16)


def dot(left, right):
    return jnp.dot(left, right, preferred_element_type=F32)


def dot_nt(left, right):
    return lax.dot_general(left, right, (((1,), (1,)), ((), ())), preferred_element_type=F32)


def product(left, right):
    lh, ll = split(left)
    rh, rl = split(right)
    return dot(lh, rh) + dot(lh, rl) + dot(ll, rh)


def kernel(
    e_hbm, v_hbm, f_hbm, out_hbm,
    e, raw, eh, el, vt, vn,
    wloc, x_land, zs, z_land, red, ag_land, wfull,
    ms, mz_land, mz, mx_land, mats,
    gacc, gloc, gz_land, gq, gx_land,
    s_stack, s_low,
    load_sem, out_sem, recv, send, sib,
    direct, x_s, x_r, z_s, z_r, ag_s, ag_r,
    ms_s, ms_r, mz_s, mz_r, mx_s, mx_r,
    gz_s, gz_r, gx_s, gx_r,
):
    row = lax.axis_index("row")
    col = lax.axis_index("col")
    z, x = row // NX, row % NX
    y, core = col // 2, col % 2

    def ring(yy, cc):
        return (row, yy * 2 + cc)

    def z_peer(d):
        return (lax.rem(z + d, NZ) * NX + x, col)

    def x_peer(d):
        return (z * NX + lax.rem(x + d, NX), col)

    at_root = y == 0
    first = ((core == 1) & (y == 1)) | ((core == 0) & (y == 3))
    last = ((core == 1) & (y == 3)) | ((core == 0) & (y == 1))
    ahead = jnp.where(core == 1, y + 1, y - 1)
    behind = jnp.where(core == 1, y - 1, y + 1)
    lag = jnp.where(first, 4, jnp.where(y == 2, 2, 1))
    mine = 1 - core
    rank = x * NZ + z

    def remote(src, dst, send_sem, recv_sem, device):
        return pltpu.make_async_remote_copy(
            src_ref=src, dst_ref=dst, send_sem=send_sem, recv_sem=recv_sem, device_id=device, device_id_type=MESH
        )

    load_e = pltpu.make_async_copy(e_hbm, e, load_sem.at[0])
    load_v = pltpu.make_async_copy(v_hbm, raw, load_sem.at[1])
    load_f = pltpu.make_async_copy(
        f_hbm.at[0, pl.ds(pl.multiple_of(rank * 8, 8), 8), :], ms.at[1 - core], load_sem.at[2]
    )

    @pl.when(at_root)
    def _():
        load_v.start()
        load_f.start()

    load_e.start()

    barrier = pltpu.get_barrier_semaphore()

    def greet(device):
        pl.semaphore_signal(barrier, inc=1, device_id=device, device_id_type=MESH)

    for d in range(1, NZ):
        greet(z_peer(d))
    for d in range(1, NX):
        greet(x_peer(d))
    greet(ring(y, 1 - core))

    @pl.when(jnp.logical_not(at_root))
    def _():
        greet(ring(0, 0))
        greet(ring(0, 1))

    @pl.when(jnp.logical_not(at_root | first))
    def _():
        greet(ring(behind, core))

    def transpose_in(ct):
        panel = 1 - core

        def body(rt, _):
            start = pl.multiple_of(rt * TILE, TILE)
            for h in range(2):
                block = raw[pl.ds(pl.multiple_of(h * HALF + start, TILE), TILE), ct * TILE : (ct + 1) * TILE]
                vt[panel, h, ct * TILE : (ct + 1) * TILE, pl.ds(start, TILE)] = block.T
            return 0

        lax.fori_loop(0, HALF // TILE, body, 0)

    @pl.when(at_root)
    def _():
        load_v.wait()
        load_f.wait()
        transpose_in(0)

    pl.semaphore_wait(barrier, (NZ - 1) + (NX - 1) + jnp.where(at_root, 7, jnp.where(last, 1, 2)))

    def spread(m):
        for d in range(1, NCOL):
            yield remote(ms.at[m], ms.at[m], ms_s.at[m], ms_r.at[m], (row, lax.rem(col + d, NCOL)))

    for m in range(2):

        @pl.when(at_root & (core == 1 - m))
        def _():
            for copy in spread(m):
                copy.start()

    def row0(g):
        return pl.multiple_of(jnp.where(g < PER_PANEL, g, GROUPS - 1 - g) * GROUP, GROUP)

    def chunk(k, h):
        g = k // TICKS
        start = pl.multiple_of(row0(g) + (k % TICKS) * TICK, TICK)
        return vt.at[g // PER_PANEL, h, pl.ds(start, TICK), :]

    def piece(k, h, send_sem, device):
        ref = chunk(k, h)
        return remote(ref, ref, send_sem, recv.at[h, k], device)

    def ring_send(k, h):
        return piece(k, h, send.at[h, k], ring(jnp.where(h == 0, 1, 3), jnp.where(h == 0, 1, 0)))

    def direct_send(k, h):
        return piece(k, h, direct.at[h, k - DIRECT], ring(jnp.where(h == 0, 3, 1), jnp.where(h == 0, 1, 0)))

    def relays(k):
        return jnp.logical_not(last | ((y == 2) & (k >= DIRECT)))

    def sib_send(k, h):
        return piece(k, h, sib.at[h, k], ring(y, 1 - core))

    def ahead_send(k):
        return piece(k, mine, send.at[0, k], ring(ahead, core))

    def pass_on(k):
        return piece(k, mine, sib.at[0, k], ring(y, 1 - core))

    def arrived(k, h):
        piece(k, h, send.at[0, k], ring(y, 1 - core)).wait_recv()

    def ticks(i, begin, end):
        owner = at_root & ((core == 1) == (i < PER_PANEL))
        follower = at_root & ((core == 0) == (i < PER_PANEL))

        for t in range(begin, end):
            k = i * TICKS + t

            @pl.when(owner)
            def _():
                @pl.when(k % (CHUNKS // 2) >= DEPTH)
                def _():
                    for h in range(2):
                        ring_send(k - DEPTH, h).wait_send()

                for h in range(2):
                    ring_send(k, h).start()

                @pl.when(k >= DIRECT)
                def _():
                    for h in range(2):
                        direct_send(k, h).start()

                for h in range(2):
                    sib_send(k, h).start()

            @pl.when(follower)
            def _():
                arrived(k, 0)
                arrived(k, 1)

            @pl.when(jnp.logical_not(at_root))
            def _():
                arrived(k, mine)

                @pl.when(relays(k))
                def _():
                    ahead_send(k).start()

                pass_on(k).start()

    def share(u):
        return 8 if isinstance(u, int) and u >= GROUPS - 1 else 16

    def first_column(u):
        if isinstance(u, int) and u == GROUPS:
            return 32
        return row0(jnp.int32(u) if isinstance(u, int) else u)

    def panel_of(u):
        return 1 if isinstance(u, int) and u >= PER_PANEL else u // PER_PANEL

    def part(ref, u):
        return ref.at[u] if share(u) == 16 else ref.at[u, :, pl.ds(0, 8), :]

    def own(u, position):
        return pl.ds(pl.multiple_of(position * share(u), 8), share(u))

    def to_x(u):
        for d in range(1, NX):
            yield remote(
                wloc.at[u, own(u, lax.rem(x + d, NX)), :],
                x_land.at[u, d - 1, pl.ds(0, share(u)), :], x_s.at[u], x_r.at[u], x_peer(d),
            )

    def to_z(u):
        for d in range(1, NZ):
            ref = zs.at[u, pl.ds(0, share(u)), :]
            yield remote(ref, z_land.at[u, d - 1, pl.ds(0, share(u)), :], z_s.at[u], z_r.at[u], z_peer(d))

    def back_x(u):
        for d in range(1, NX):
            ref = red.at[u, pl.ds(0, share(u)), :]
            yield remote(ref, ag_land.at[u, d - 1, pl.ds(0, share(u)), :], ag_s.at[u], ag_r.at[u], x_peer(d))

    def whole(ref, send_sem, recv_sem):
        return remote(ref, ref, send_sem, recv_sem, ring(y, 1 - core))

    def project(u):
        count = share(u) * NX
        total = jnp.zeros((count, NB), F32)
        for h in range(2):
            high, low = split(vt[panel_of(u), h, pl.ds(first_column(u), count), :])
            both = dot(jnp.concatenate([high, low], axis=0), eh[h * HALF : (h + 1) * HALF, :])
            total += both[:count] + both[count:] + dot(high, el[h * HALF : (h + 1) * HALF, :])
        wloc[u, :count] = total
        for copy in to_x(u):
            copy.start()

    def sum_x(u):
        n = share(u)
        whole(part(x_land, u), x_s.at[u], x_r.at[u]).wait_recv()
        total = wloc[u, own(u, x), :]
        for d in range(NX - 1):
            total += x_land[u, d, :n]
        zs[u, :n] = total
        for copy in to_z(u):
            copy.start()

    def sum_z(u):
        n = share(u)
        whole(part(z_land, u), z_s.at[u], z_r.at[u]).wait_recv()
        total = zs[u, :n]
        for d in range(NZ - 1):
            total += z_land[u, d, :n]
        red[u, :n] = total
        for copy in back_x(u):
            copy.start()

    def gather(u):
        n = share(u)
        whole(part(ag_land, u), ag_s.at[u], ag_r.at[u]).wait_recv()
        base = panel_of(u) * NB + first_column(u)
        wfull[pl.ds(pl.multiple_of(base + x * n, 8), n), :] = red[u, :n]
        for d in range(1, NX):
            origin = lax.rem(x + NX - d, NX)
            wfull[pl.ds(pl.multiple_of(base + origin * n, 8), n), :] = ag_land[u, d - 1, :n]

    def tile_column(j):
        return pl.multiple_of(jnp.where((j == 1) | (j == 2), TILE, 0), TILE)

    def transpose_out(j, h):
        def body(rt, _):
            start = pl.multiple_of(rt * TILE, TILE)
            block = vt[j // 2, h, pl.ds(tile_column(j), TILE), pl.ds(start, TILE)]
            high, low = split(block.T)
            rows = pl.ds(pl.multiple_of(h * HALF + start, TILE), TILE)
            vn[j, rows, :TILE] = high
            vn[j, rows, TILE:] = low
            return 0

        lax.fori_loop(0, HALF // TILE, body, 0)

    def m_to_z(m):
        for d in range(1, NZ):
            yield remote(ms.at[m], mz_land.at[m, d - 1], mz_s.at[m], mz_r.at[m], z_peer(d))

    def m_to_x(m):
        for d in range(1, NX):
            yield remote(mz.at[m], mx_land.at[m, d - 1], mx_s.at[m], mx_r.at[m], x_peer(d))

    def m_begin(m):
        is_source = at_root & ((core == 1) if m == 0 else (core == 0))

        @pl.when(jnp.logical_not(is_source))
        def _():
            whole(ms.at[m], ms_s.at[m], ms_r.at[m]).wait_recv()

        for copy in m_to_z(m):
            copy.start()

    def m_middle(m):
        whole(mz_land.at[m], mz_s.at[m], mz_r.at[m]).wait_recv()
        mz[m, pl.ds(pl.multiple_of(z * 8, 8), 8), :] = ms[m]
        for d in range(1, NZ):
            origin = lax.rem(z + NZ - d, NZ)
            mz[m, pl.ds(pl.multiple_of(origin * 8, 8), 8), :] = mz_land[m, d - 1]
        for copy in m_to_x(m):
            copy.start()

    def m_end(m):
        whole(mx_land.at[m], mx_s.at[m], mx_r.at[m]).wait_recv()
        mats[m, pl.ds(pl.multiple_of(x * 64, 64), 64), :] = mz[m]
        for d in range(1, NX):
            origin = lax.rem(x + NX - d, NX)
            mats[m, pl.ds(pl.multiple_of(origin * 64, 64), 64), :] = mx_land[m, d - 1]

    overlap_here = at_root & (core == 0)

    def overlap_to_z():
        for d in range(1, NZ):
            yield remote(gloc.at[lax.rem(z + d, NZ)], gz_land.at[d - 1], gz_s.at[0], gz_r.at[0], z_peer(d))

    def overlap_to_x():
        for d in range(1, NX):
            yield remote(gq.at[lax.rem(x + d, NX)], gx_land.at[d - 1], gx_s.at[0], gx_r.at[0], x_peer(d))

    def overlap_begin():
        gacc[...] = jnp.zeros_like(gacc)

        def body(n, _):
            h, part = n // 3, n % 3
            lanes = pl.ds(pl.multiple_of(part * 512, 512), 512)
            ah, al = split(vt[1, h, :, lanes])
            bh, bl = split(vt[0, h, :, lanes])
            gacc[...] += dot_nt(ah, bh) + dot_nt(ah, bl) + dot_nt(al, bh)
            return 0

        lax.fori_loop(0, 6, body, 0)
        for zz in range(NZ):
            for xx in range(NX):
                gloc[zz, xx] = gacc[xx * 64 + zz * 8 : xx * 64 + zz * 8 + 8, :]
        for copy in overlap_to_z():
            copy.start()

    def overlap_middle():
        whole(gz_land, gz_s.at[0], gz_r.at[0]).wait_recv()
        total = gloc[z]
        for d in range(NZ - 1):
            total += gz_land[d]
        gq[...] = total
        for copy in overlap_to_x():
            copy.start()

    def overlap_end():
        whole(gx_land, gx_s.at[0], gx_r.at[0]).wait_recv()
        total = gq[x]
        for d in range(NX - 1):
            total += gx_land[d]
        ms[2] = total
        for copy in spread(2):
            copy.start()

    def split_field():
        load_e.wait()

        def body(n, _):
            rows = pl.ds(pl.multiple_of(n * 256, 256), 256)
            high, low = split(e[rows, :])
            eh[rows, :] = high
            el[rows, :] = low
            return 0

        lax.fori_loop(0, ROWS // 256, body, 0)

    def when(condition, action, *args):
        pl.when(condition)(lambda: action(*args))

    def other_half(done, begin, end):
        @pl.when(jnp.logical_not(at_root))
        def _():
            for t in range(begin, end):
                arrived(done * TICKS + t, core)

    def step(i, _):
        done = i - lag
        when(i < GROUPS, ticks, i, 0, 1)

        @pl.when(i == 0)
        def _():
            when(at_root, transpose_in, 1)

        @pl.when(done >= 0)
        def _():
            other_half(done, 0, TICKS)
            project(done)

        when(i < GROUPS, ticks, i, 1, 2)
        when(done >= 1, sum_x, done - 1)
        when(done >= 3, sum_z, done - 3)
        when(i < GROUPS, ticks, i, 2, 3)

        @pl.when((i == GROUPS - 1) & last)
        def _():
            other_half(GROUPS - 1, 0, TICKS // 2)
            project(GROUPS - 1)

        when(i == 0, split_field)
        when(done >= 1, lambda: transpose_out((done - 1) // 2, (done - 1) % 2))
        when(i < GROUPS, ticks, i, 3, 4)

        @pl.when(done == 1)
        def _():
            m_begin(0)
            m_begin(1)

        @pl.when(done == 3)
        def _():
            m_middle(0)
            m_middle(1)

        when(overlap_here & (i == 4), overlap_begin)
        when(overlap_here & (i == 6), overlap_middle)
        when(overlap_here & (i == 7), overlap_end)
        when(done == 6, m_begin, 2)
        return 0

    lax.fori_loop(0, GROUPS - 1 + lag, step, 0)

    @pl.when(jnp.logical_not(last))
    def _():
        other_half(GROUPS - 1, 0, TICKS // 2)
        project(GROUPS - 1)

    other_half(GROUPS - 1, TICKS // 2, TICKS)
    project(GROUPS)

    def set_s(j, value):
        high, low = split(value)
        s_stack[j, :TILE] = high
        s_stack[j, TILE:] = high
        s_low[j] = low

    def update(tiles, finish):
        def body(n, _):
            rows = pl.ds(pl.multiple_of(n * 512, 512), 512)
            total = e[rows, :]
            for j in tiles:
                part = vn[j, rows, :]
                total -= dot(part, s_stack[j]) + dot(part[:, :TILE], s_low[j])
            e[rows, :] = total
            if finish:
                pltpu.make_async_copy(e.at[rows], out_hbm.at[rows], out_sem.at[n]).start()
            return 0

        lax.fori_loop(0, ROWS // 512, body, 0)

    sum_x(6)
    sum_z(4)
    transpose_out(3, 0)
    sum_x(7)
    sum_x(8)
    sum_z(5)
    m_end(0)
    m_end(1)
    transpose_out(3, 1)
    m_middle(2)
    for u in range(4):
        gather(u)
    first_s = product(mats[0], wfull[:NB, :])
    set_s(0, first_s[:TILE])
    set_s(1, first_s[TILE:])
    sum_z(6)
    update((0, 1), False)
    sum_z(7)
    sum_z(8)
    gather(4)
    gather(5)
    m_end(2)
    correction = product(mats[2], first_s)
    upper = wfull[NB + TILE :, :] - correction[TILE:]
    set_s(2, product(mats[1, TILE:, TILE:], upper))
    update((2,), False)
    gather(6)
    gather(7)
    gather(8)
    lower = wfull[NB : NB + TILE, :] - correction[:TILE]
    set_s(3, product(mats[1, :TILE, :], jnp.concatenate([lower, upper], axis=0)))
    update((3,), True)

    for u in range(UNITS):
        whole(part(x_land, u), x_s.at[u], x_r.at[u]).wait_send()
        whole(part(z_land, u), z_s.at[u], z_r.at[u]).wait_send()
        whole(part(ag_land, u), ag_s.at[u], ag_r.at[u]).wait_send()
    for m in range(3):
        whole(mz_land.at[m], mz_s.at[m], mz_r.at[m]).wait_send()
        whole(mx_land.at[m], mx_s.at[m], mx_r.at[m]).wait_send()

        @pl.when(at_root & ((core == 1) if m == 0 else (core == 0)))
        def _():
            whole(mz_land.at[m], ms_s.at[m], ms_r.at[m]).wait_send()

    @pl.when(overlap_here)
    def _():
        whole(gz_land, gz_s.at[0], gz_r.at[0]).wait_send()
        whole(gx_land, gx_s.at[0], gx_r.at[0]).wait_send()

    def drain(k, _):
        @pl.when(jnp.logical_not(at_root))
        def _():
            @pl.when(relays(k))
            def _():
                ahead_send(k).wait_send()

            pass_on(k).wait_send()

        @pl.when(at_root & ((core == 1) == (k < CHUNKS // 2)))
        def _():
            for h in range(2):
                sib_send(k, h).wait_send()

                @pl.when(k % (CHUNKS // 2) >= CHUNKS // 2 - DEPTH)
                def _():
                    ring_send(k, h).wait_send()

                @pl.when(k >= DIRECT)
                def _():
                    direct_send(k, h).wait_send()

        return 0

    lax.fori_loop(0, CHUNKS, drain, 0)

    def finish(n, _):
        rows = pl.ds(pl.multiple_of(n * 512, 512), 512)
        pltpu.make_async_copy(e.at[rows], out_hbm.at[rows], out_sem.at[n]).wait()
        return 0

    lax.fori_loop(0, ROWS // 512, finish, 0)


def local(eigvecs, reflectors, factors):
    vmem, dma = pltpu.VMEM, pltpu.SemaphoreType.DMA
    anywhere = pl.BlockSpec(memory_space=pl.ANY)
    return pl.pallas_call(
        kernel,
        out_shape=jax.ShapeDtypeStruct((ROWS, NB), F32),
        in_specs=[pl.BlockSpec(memory_space=pltpu.HBM)] * 3,
        out_specs=anywhere,
        scratch_shapes=[
            vmem((ROWS, NB), F32),
            vmem((ROWS, NB), F32),
            vmem((ROWS, NB), BF16),
            vmem((ROWS, NB), BF16),
            vmem((2, 2, NB, HALF), F32),
            vmem((4, ROWS, NB), BF16),
            vmem((UNITS, GROUP, NB), F32),
            vmem((UNITS, NX - 1, 16, NB), F32),
            vmem((UNITS, 16, NB), F32),
            vmem((UNITS, NZ - 1, 16, NB), F32),
            vmem((UNITS, 16, NB), F32),
            vmem((UNITS, NX - 1, 16, NB), F32),
            vmem((2 * NB, NB), F32),
            vmem((3, 8, NB), F32),
            vmem((3, NZ - 1, 8, NB), F32),
            vmem((3, 64, NB), F32),
            vmem((3, NX - 1, 64, NB), F32),
            vmem((3, NB, NB), F32),
            vmem((NB, NB), F32),
            vmem((NZ, NX, 8, NB), F32),
            vmem((NZ - 1, NX, 8, NB), F32),
            vmem((NX, 8, NB), F32),
            vmem((NX - 1, 8, NB), F32),
            vmem((4, NB, NB), BF16),
            vmem((4, TILE, NB), BF16),
            dma((3,)),
            dma((ROWS // 512,)),
            dma((2, CHUNKS)),
            dma((2, CHUNKS)),
            dma((2, CHUNKS)),
            dma((2, CHUNKS - DIRECT)),
            *[dma((UNITS,))] * 6,
            *[dma((3,))] * 6,
            *[dma((1,))] * 4,
        ],
        compiler_params=pltpu.CompilerParams(collective_id=0, has_side_effects=True, vmem_limit_bytes=50 * 2**20),
    )(eigvecs, reflectors, factors)


def solution(mesh):
    in_specs = (P("row", "col"), P("row", "col"), P("col", None, None))
    return jax.shard_map(local, mesh=mesh, in_specs=in_specs, out_specs=P("row", "col"), check_vma=False)
```

```python
import jax
import jax.numpy as jnp
from jax import lax
from jax.experimental import pallas as pl
from jax.experimental.pallas import tpu as pltpu
from jax.sharding import PartitionSpec as P

MESH = pl.DeviceIdType.MESH
F32, BF16 = jnp.float32, jnp.bfloat16
NZ, NX, NCOL = 8, 4, 8
NB = 256
ROWS = 3072
HALF = ROWS // 2
TICK = 16
GROUP = 64
TICKS = GROUP // TICK
PER_PANEL = NB // GROUP
GROUPS = 2 * PER_PANEL
CHUNKS = GROUPS * TICKS
TILE = 128
DEPTH = 3
DIRECT = CHUNKS - 2
UNITS = GROUPS + 1


def split(value):
    high = value.astype(BF16)
    return high, (value - high.astype(F32)).astype(BF16)


def dot(left, right):
    return jnp.dot(left, right, preferred_element_type=F32)


def dot_nt(left, right):
    return lax.dot_general(left, right, (((1,), (1,)), ((), ())), preferred_element_type=F32)


def product(left, right):
    lh, ll = split(left)
    rh, rl = split(right)
    return dot(lh, rh) + dot(lh, rl) + dot(ll, rh)


def kernel(
    e_hbm, v_hbm, f_hbm, out,
    e, raw, eh, el, vt, vn,
    wloc, x_land, zs, z_land, red, ag_land, wfull,
    ms, mz_land, mz, mx_land, mats,
    gacc, gloc, gz_land, gq, gx_land,
    s_stack, s_low,
    known, load_sem, recv, send, sib,
    direct, x_s, x_r, z_s, z_r, ag_s, ag_r,
    ms_s, ms_r, mz_s, mz_r, mx_s, mx_r,
    gz_s, gz_r, gx_s, gx_r,
):
    row = lax.axis_index("row")
    col = lax.axis_index("col")
    z, x = row // NX, row % NX
    y, core = col // 2, col % 2

    def ring(yy, cc):
        return (row, yy * 2 + cc)

    def z_peer(d):
        return (lax.rem(z + d, NZ) * NX + x, col)

    def x_peer(d):
        return (z * NX + lax.rem(x + d, NX), col)

    at_root = y == 0
    first = ((core == 1) & (y == 1)) | ((core == 0) & (y == 3))
    last = ((core == 1) & (y == 3)) | ((core == 0) & (y == 1))
    ahead = jnp.where(core == 1, y + 1, y - 1)
    behind = jnp.where(core == 1, y - 1, y + 1)
    lag = jnp.where(first, 4, jnp.where(y == 2, 2, 1))
    mine = 1 - core
    rank = x * NZ + z

    def remote(src, dst, send_sem, recv_sem, device):
        return pltpu.make_async_remote_copy(
            src_ref=src, dst_ref=dst, send_sem=send_sem, recv_sem=recv_sem, device_id=device, device_id_type=MESH
        )

    load_e = pltpu.make_async_copy(e_hbm, e, load_sem.at[0])
    load_v = pltpu.make_async_copy(v_hbm, raw, load_sem.at[1])
    load_f = pltpu.make_async_copy(
        f_hbm.at[0, pl.ds(pl.multiple_of(rank * 8, 8), 8), :], ms.at[1 - core], load_sem.at[2]
    )

    @pl.when(at_root)
    def _():
        load_v.start()
        load_f.start()

    load_e.start()

    barrier = pltpu.get_barrier_semaphore()

    def greet(device):
        pl.semaphore_signal(barrier, inc=1, device_id=device, device_id_type=MESH)

    neighbours = (z_peer(1), z_peer(NZ - 1), x_peer(1), x_peer(NX - 1), ring(y, 1 - core))
    for device in neighbours:
        greet(device)

    @pl.when(y % 2 == 1)
    def _():
        greet(ring(0, 0))
        greet(ring(0, 1))

    @pl.when(jnp.logical_not(at_root | first))
    def _():
        greet(ring(behind, core))

    def transpose_in(ct):
        panel = 1 - core

        def body(rt, _):
            start = pl.multiple_of(rt * TILE, TILE)
            for h in range(2):
                block = raw[pl.ds(pl.multiple_of(h * HALF + start, TILE), TILE), ct * TILE : (ct + 1) * TILE]
                vt[panel, h, ct * TILE : (ct + 1) * TILE, pl.ds(start, TILE)] = block.T
            return 0

        lax.fori_loop(0, HALF // TILE, body, 0)

    @pl.when(at_root)
    def _():
        load_v.wait()
        load_f.wait()
        transpose_in(0)

    pl.semaphore_wait(barrier, len(neighbours) + jnp.where(at_root, 4, jnp.where(last, 0, 1)))

    def tell(n):
        pl.semaphore_signal(known.at[n, 0], inc=1, device_id=z_peer(1), device_id_type=MESH)
        pl.semaphore_signal(known.at[n, 1], inc=1, device_id=z_peer(NZ - 1), device_id_type=MESH)
        if n == 0:
            pl.semaphore_signal(known.at[n, 2], inc=1, device_id=x_peer(1), device_id_type=MESH)

    def hear(n):
        for which in range(3 if n == 0 else 2):
            pl.semaphore_wait(known.at[n, which], 1)

    tell(0)

    def spread(m):
        for device in (ring(0, 1 - core), ring(1, 0), ring(1, 1), ring(3, 0), ring(3, 1)):
            yield remote(ms.at[m], ms.at[m], ms_s.at[m], ms_r.at[m], device)

    def spread_on(m):
        return remote(ms.at[m], ms.at[m], ms_s.at[m], ms_r.at[m], ring(2, core))

    for m in range(2):

        @pl.when(at_root & (core == 1 - m))
        def _():
            for copy in spread(m):
                copy.start()

    def row0(g):
        return pl.multiple_of(jnp.where(g < PER_PANEL, g, GROUPS - 1 - g) * GROUP, GROUP)

    def chunk(k, h):
        g = k // TICKS
        start = pl.multiple_of(row0(g) + (k % TICKS) * TICK, TICK)
        return vt.at[g // PER_PANEL, h, pl.ds(start, TICK), :]

    def piece(k, h, send_sem, device):
        ref = chunk(k, h)
        return remote(ref, ref, send_sem, recv.at[h, k], device)

    def ring_send(k, h):
        return piece(k, h, send.at[h, k], ring(jnp.where(h == 0, 1, 3), jnp.where(h == 0, 1, 0)))

    def direct_send(k, h):
        return piece(k, h, direct.at[h, k - DIRECT], ring(jnp.where(h == 0, 3, 1), jnp.where(h == 0, 1, 0)))

    def relays(k):
        return jnp.logical_not(last | ((y == 2) & (k >= DIRECT)))

    def sib_send(k, h):
        return piece(k, h, sib.at[h, k], ring(y, 1 - core))

    def ahead_send(k):
        return piece(k, mine, send.at[0, k], ring(ahead, core))

    def pass_on(k):
        return piece(k, mine, sib.at[0, k], ring(y, 1 - core))

    def arrived(k, h):
        piece(k, h, send.at[0, k], ring(y, 1 - core)).wait_recv()

    def ticks(i, begin, end):
        owner = at_root & ((core == 1) == (i < PER_PANEL))
        follower = at_root & ((core == 0) == (i < PER_PANEL))

        for t in range(begin, end):
            k = i * TICKS + t

            @pl.when(owner)
            def _():
                @pl.when(k % (CHUNKS // 2) >= DEPTH)
                def _():
                    for h in range(2):
                        ring_send(k - DEPTH, h).wait_send()

                for h in range(2):
                    ring_send(k, h).start()

                @pl.when(k >= DIRECT)
                def _():
                    for h in range(2):
                        direct_send(k, h).start()

                for h in range(2):
                    sib_send(k, h).start()

            @pl.when(follower)
            def _():
                arrived(k, 0)
                arrived(k, 1)

            @pl.when(jnp.logical_not(at_root))
            def _():
                arrived(k, mine)

                @pl.when(relays(k))
                def _():
                    ahead_send(k).start()

                pass_on(k).start()

    def share(u):
        return 8 if isinstance(u, int) and u >= GROUPS - 1 else 16

    def first_column(u):
        if isinstance(u, int) and u == GROUPS:
            return 32
        return row0(jnp.int32(u) if isinstance(u, int) else u)

    def panel_of(u):
        return 1 if isinstance(u, int) and u >= PER_PANEL else u // PER_PANEL

    def part(ref, u):
        return ref.at[u] if share(u) == 16 else ref.at[u, :, pl.ds(0, 8), :]

    def own(u, position):
        return pl.ds(pl.multiple_of(position * share(u), 8), share(u))

    def to_x(u):
        for d in range(1, NX):
            yield remote(
                wloc.at[u, own(u, lax.rem(x + d, NX)), :],
                x_land.at[u, d - 1, pl.ds(0, share(u)), :], x_s.at[u], x_r.at[u], x_peer(d),
            )

    def to_z(u):
        for d in range(1, NZ):
            ref = zs.at[u, pl.ds(0, share(u)), :]
            yield remote(ref, z_land.at[u, d - 1, pl.ds(0, share(u)), :], z_s.at[u], z_r.at[u], z_peer(d))

    def back_x(u):
        for d in range(1, NX):
            ref = red.at[u, pl.ds(0, share(u)), :]
            yield remote(ref, ag_land.at[u, d - 1, pl.ds(0, share(u)), :], ag_s.at[u], ag_r.at[u], x_peer(d))

    def whole(ref, send_sem, recv_sem):
        return remote(ref, ref, send_sem, recv_sem, ring(y, 1 - core))

    def project(u):
        count = share(u) * NX
        total = jnp.zeros((count, NB), F32)
        for h in range(2):
            high, low = split(vt[panel_of(u), h, pl.ds(first_column(u), count), :])
            both = dot(jnp.concatenate([high, low], axis=0), eh[h * HALF : (h + 1) * HALF, :])
            total += both[:count] + both[count:] + dot(high, el[h * HALF : (h + 1) * HALF, :])
        wloc[u, :count] = total
        for copy in to_x(u):
            copy.start()

    def sum_x(u):
        n = share(u)
        whole(part(x_land, u), x_s.at[u], x_r.at[u]).wait_recv()
        total = wloc[u, own(u, x), :]
        for d in range(NX - 1):
            total += x_land[u, d, :n]
        zs[u, :n] = total
        for copy in to_z(u):
            copy.start()

    def sum_z(u):
        n = share(u)
        whole(part(z_land, u), z_s.at[u], z_r.at[u]).wait_recv()
        total = zs[u, :n]
        for d in range(NZ - 1):
            total += z_land[u, d, :n]
        red[u, :n] = total
        for copy in back_x(u):
            copy.start()

    def gather(u):
        n = share(u)
        whole(part(ag_land, u), ag_s.at[u], ag_r.at[u]).wait_recv()
        base = panel_of(u) * NB + first_column(u)
        wfull[pl.ds(pl.multiple_of(base + x * n, 8), n), :] = red[u, :n]
        for d in range(1, NX):
            origin = lax.rem(x + NX - d, NX)
            wfull[pl.ds(pl.multiple_of(base + origin * n, 8), n), :] = ag_land[u, d - 1, :n]

    def tile_column(j):
        return pl.multiple_of(jnp.where((j == 1) | (j == 2), TILE, 0), TILE)

    def transpose_out(j, h):
        def body(rt, _):
            start = pl.multiple_of(rt * TILE, TILE)
            block = vt[j // 2, h, pl.ds(tile_column(j), TILE), pl.ds(start, TILE)]
            high, low = split(block.T)
            rows = pl.ds(pl.multiple_of(h * HALF + start, TILE), TILE)
            vn[j, rows, :TILE] = high
            vn[j, rows, TILE:] = low
            return 0

        lax.fori_loop(0, HALF // TILE, body, 0)

    def m_to_z(m):
        for d in range(1, NZ):
            yield remote(ms.at[m], mz_land.at[m, d - 1], mz_s.at[m], mz_r.at[m], z_peer(d))

    def m_to_x(m):
        for d in range(1, NX):
            yield remote(mz.at[m], mx_land.at[m, d - 1], mx_s.at[m], mx_r.at[m], x_peer(d))

    def m_begin(m):
        is_source = at_root & ((core == 1) if m == 0 else (core == 0))

        @pl.when(jnp.logical_not(is_source))
        def _():
            whole(ms.at[m], ms_s.at[m], ms_r.at[m]).wait_recv()

        @pl.when(first)
        def _():
            spread_on(m).start()

        for copy in m_to_z(m):
            copy.start()

    def m_middle(m):
        whole(mz_land.at[m], mz_s.at[m], mz_r.at[m]).wait_recv()
        mz[m, pl.ds(pl.multiple_of(z * 8, 8), 8), :] = ms[m]
        for d in range(1, NZ):
            origin = lax.rem(z + NZ - d, NZ)
            mz[m, pl.ds(pl.multiple_of(origin * 8, 8), 8), :] = mz_land[m, d - 1]
        for copy in m_to_x(m):
            copy.start()

    def m_end(m):
        whole(mx_land.at[m], mx_s.at[m], mx_r.at[m]).wait_recv()
        mats[m, pl.ds(pl.multiple_of(x * 64, 64), 64), :] = mz[m]
        for d in range(1, NX):
            origin = lax.rem(x + NX - d, NX)
            mats[m, pl.ds(pl.multiple_of(origin * 64, 64), 64), :] = mx_land[m, d - 1]

    overlap_here = at_root & (core == 0)

    def overlap_to_z():
        for d in range(1, NZ):
            yield remote(gloc.at[lax.rem(z + d, NZ)], gz_land.at[d - 1], gz_s.at[0], gz_r.at[0], z_peer(d))

    def overlap_to_x():
        for d in range(1, NX):
            yield remote(gq.at[lax.rem(x + d, NX)], gx_land.at[d - 1], gx_s.at[0], gx_r.at[0], x_peer(d))

    def overlap_begin():
        gacc[...] = jnp.zeros_like(gacc)

        def body(n, _):
            h, part = n // 3, n % 3
            lanes = pl.ds(pl.multiple_of(part * 512, 512), 512)
            ah, al = split(vt[1, h, :, lanes])
            bh, bl = split(vt[0, h, :, lanes])
            gacc[...] += dot_nt(ah, bh) + dot_nt(ah, bl) + dot_nt(al, bh)
            return 0

        lax.fori_loop(0, 6, body, 0)
        for zz in range(NZ):
            for xx in range(NX):
                gloc[zz, xx] = gacc[xx * 64 + zz * 8 : xx * 64 + zz * 8 + 8, :]
        for copy in overlap_to_z():
            copy.start()

    def overlap_middle():
        whole(gz_land, gz_s.at[0], gz_r.at[0]).wait_recv()
        total = gloc[z]
        for d in range(NZ - 1):
            total += gz_land[d]
        gq[...] = total
        for copy in overlap_to_x():
            copy.start()

    def overlap_end():
        whole(gx_land, gx_s.at[0], gx_r.at[0]).wait_recv()
        total = gq[x]
        for d in range(NX - 1):
            total += gx_land[d]
        ms[2] = total
        for copy in spread(2):
            copy.start()

    def split_field():
        load_e.wait()

        def body(n, _):
            rows = pl.ds(pl.multiple_of(n * 256, 256), 256)
            high, low = split(e[rows, :])
            eh[rows, :] = high
            el[rows, :] = low
            return 0

        lax.fori_loop(0, ROWS // 256, body, 0)

    def when(condition, action, *args):
        pl.when(condition)(lambda: action(*args))

    def other_half(done, begin, end):
        @pl.when(jnp.logical_not(at_root))
        def _():
            for t in range(begin, end):
                arrived(done * TICKS + t, core)

    def step(i, _):
        done = i - lag
        when(i < GROUPS, ticks, i, 0, 1)

        @pl.when(i == 0)
        def _():
            when(at_root, transpose_in, 1)

        @pl.when(i == 1)
        def _():
            hear(1)
            tell(2)

        @pl.when(done >= 0)
        def _():
            other_half(done, 0, TICKS)
            project(done)

        when(i < GROUPS, ticks, i, 1, 2)
        when(done >= 1, sum_x, done - 1)
        when(done >= 3, sum_z, done - 3)
        when(i < GROUPS, ticks, i, 2, 3)

        @pl.when((i == GROUPS - 1) & last)
        def _():
            other_half(GROUPS - 1, 0, TICKS // 2)
            project(GROUPS - 1)

        when(i == 0, split_field)
        when(done >= 1, lambda: transpose_out((done - 1) // 2, (done - 1) % 2))
        when(i < GROUPS, ticks, i, 3, 4)

        @pl.when(i == 0)
        def _():
            hear(0)
            tell(1)

        when(i == 1, hear, 2)

        @pl.when(done == 1)
        def _():
            m_begin(0)
            m_begin(1)

        @pl.when(done == 3)
        def _():
            m_middle(0)
            m_middle(1)

        when(overlap_here & (i == 4), overlap_begin)
        when(overlap_here & (i == 6), overlap_middle)
        when(overlap_here & (i == 7), overlap_end)
        when(done == 6, m_begin, 2)
        return 0

    lax.fori_loop(0, GROUPS - 1 + lag, step, 0)

    @pl.when(jnp.logical_not(last))
    def _():
        other_half(GROUPS - 1, 0, TICKS // 2)
        project(GROUPS - 1)

    other_half(GROUPS - 1, TICKS // 2, TICKS)
    project(GROUPS)

    def left(u):
        whole(part(x_land, u), x_s.at[u], x_r.at[u]).wait_send()
        whole(part(z_land, u), z_s.at[u], z_r.at[u]).wait_send()
        whole(part(ag_land, u), ag_s.at[u], ag_r.at[u]).wait_send()

    def matrices_left():
        for m in range(3):
            whole(mz_land.at[m], mz_s.at[m], mz_r.at[m]).wait_send()
            whole(mx_land.at[m], mx_s.at[m], mx_r.at[m]).wait_send()

            @pl.when(at_root & ((core == 1) if m == 0 else (core == 0)))
            def _():
                whole(mz_land.at[m, pl.ds(0, 5)], ms_s.at[m], ms_r.at[m]).wait_send()

            @pl.when(first)
            def _():
                spread_on(m).wait_send()

        @pl.when(overlap_here)
        def _():
            whole(gz_land, gz_s.at[0], gz_r.at[0]).wait_send()
            whole(gx_land, gx_s.at[0], gx_r.at[0]).wait_send()

    def stream_left():
        def drain(k, _):
            @pl.when(jnp.logical_not(at_root))
            def _():
                @pl.when(relays(k))
                def _():
                    ahead_send(k).wait_send()

                pass_on(k).wait_send()

            @pl.when(at_root & ((core == 1) == (k < CHUNKS // 2)))
            def _():
                for h in range(2):
                    sib_send(k, h).wait_send()

                    @pl.when(k % (CHUNKS // 2) >= CHUNKS // 2 - DEPTH)
                    def _():
                        ring_send(k, h).wait_send()

                    @pl.when(k >= DIRECT)
                    def _():
                        direct_send(k, h).wait_send()

            return 0

        lax.fori_loop(0, CHUNKS, drain, 0)

    def set_s(j, value):
        high, low = split(value)
        s_stack[j, :TILE] = high
        s_stack[j, TILE:] = high
        s_low[j] = low

    def update(tiles, target):
        def body(n, _):
            rows = pl.ds(pl.multiple_of(n * 512, 512), 512)
            total = e[rows, :]
            for j in tiles:
                part = vn[j, rows, :]
                total -= dot(part, s_stack[j]) + dot(part[:, :TILE], s_low[j])
            target[rows, :] = total
            return 0

        lax.fori_loop(0, ROWS // 512, body, 0)

    sum_x(6)
    sum_z(4)
    transpose_out(3, 0)
    sum_x(7)
    sum_x(8)
    sum_z(5)
    m_end(0)
    m_end(1)
    transpose_out(3, 1)
    m_middle(2)
    for u in range(4):
        gather(u)
    first_s = product(mats[0], wfull[:NB, :])
    set_s(0, first_s[:TILE])
    set_s(1, first_s[TILE:])
    sum_z(6)
    stream_left()
    sum_z(7)
    sum_z(8)
    update((0, 1), e)
    gather(4)
    gather(5)
    m_end(2)
    correction = product(mats[2], first_s)
    upper = wfull[NB + TILE :, :] - correction[TILE:]
    set_s(2, product(mats[1, TILE:, TILE:], upper))
    update((2,), e)
    matrices_left()
    for u in range(UNITS):
        left(u)
    gather(6)
    gather(7)
    gather(8)
    lower = wfull[NB : NB + TILE, :] - correction[:TILE]
    set_s(3, product(mats[1, :TILE, :], jnp.concatenate([lower, upper], axis=0)))
    update((3,), out)


def local(eigvecs, reflectors, factors):
    vmem, dma = pltpu.VMEM, pltpu.SemaphoreType.DMA
    return pl.pallas_call(
        kernel,
        out_shape=jax.ShapeDtypeStruct((ROWS, NB), F32),
        in_specs=[pl.BlockSpec(memory_space=pltpu.HBM)] * 3,
        out_specs=pl.BlockSpec(memory_space=pltpu.VMEM),
        scratch_shapes=[
            vmem((ROWS, NB), F32),
            vmem((ROWS, NB), F32),
            vmem((ROWS, NB), BF16),
            vmem((ROWS, NB), BF16),
            vmem((2, 2, NB, HALF), F32),
            vmem((4, ROWS, NB), BF16),
            vmem((UNITS, GROUP, NB), F32),
            vmem((UNITS, NX - 1, 16, NB), F32),
            vmem((UNITS, 16, NB), F32),
            vmem((UNITS, NZ - 1, 16, NB), F32),
            vmem((UNITS, 16, NB), F32),
            vmem((UNITS, NX - 1, 16, NB), F32),
            vmem((2 * NB, NB), F32),
            vmem((3, 8, NB), F32),
            vmem((3, NZ - 1, 8, NB), F32),
            vmem((3, 64, NB), F32),
            vmem((3, NX - 1, 64, NB), F32),
            vmem((3, NB, NB), F32),
            vmem((NB, NB), F32),
            vmem((NZ, NX, 8, NB), F32),
            vmem((NZ - 1, NX, 8, NB), F32),
            vmem((NX, 8, NB), F32),
            vmem((NX - 1, 8, NB), F32),
            vmem((4, NB, NB), BF16),
            vmem((4, TILE, NB), BF16),
            pltpu.SemaphoreType.REGULAR((3, 3)),
            dma((3,)),
            dma((2, CHUNKS)),
            dma((2, CHUNKS)),
            dma((2, CHUNKS)),
            dma((2, CHUNKS - DIRECT)),
            *[dma((UNITS,))] * 6,
            *[dma((3,))] * 6,
            *[dma((1,))] * 4,
        ],
        compiler_params=pltpu.CompilerParams(collective_id=0, has_side_effects=True, vmem_limit_bytes=50 * 2**20),
    )(eigvecs, reflectors, factors)


def solution(mesh):
    in_specs = (P("row", "col"), P("row", "col"), P("col", None, None))
    return jax.shard_map(local, mesh=mesh, in_specs=in_specs, out_specs=P("row", "col"), check_vma=False)
```

```python
import jax
import jax.numpy as jnp
from jax import lax
from jax.experimental import pallas as pl
from jax.experimental.pallas import tpu as pltpu
from jax.sharding import PartitionSpec as P

MESH = pl.DeviceIdType.MESH
F32, BF16 = jnp.float32, jnp.bfloat16
NZ, NX, NCOL = 8, 4, 8
NB = 256
ROWS = 3072
HALF = ROWS // 2
TICK = 16
GROUP = 64
TICKS = GROUP // TICK
PER_PANEL = NB // GROUP
GROUPS = 2 * PER_PANEL
CHUNKS = GROUPS * TICKS
TILE = 128
DEPTH = 3
DIRECT = CHUNKS - 2
UNITS = GROUPS + 1


def split(value):
    high = value.astype(BF16)
    return high, (value - high.astype(F32)).astype(BF16)


def dot(left, right):
    return jnp.dot(left, right, preferred_element_type=F32)


def dot_nt(left, right):
    return lax.dot_general(left, right, (((1,), (1,)), ((), ())), preferred_element_type=F32)


def product(left, right):
    lh, ll = split(left)
    rh, rl = split(right)
    return dot(lh, rh) + dot(lh, rl) + dot(ll, rh)


def kernel(
    e_hbm, v_hbm, f_hbm, out,
    e, raw, eh, el, vt, vn,
    wloc, x_land, zs, z_land, red, ag_land, wfull,
    ms, mz_land, mz, mx_land, mats,
    gacc, gloc, gz_land, gq, gx_land,
    known, load_sem, recv, send, sib, passed,
    direct, x_s, x_r, z_s, z_r, ag_s, ag_r,
    ms_s, ms_r, mz_s, mz_r, mx_s, mx_r,
    gz_s, gz_r, gx_s, gx_r,
):
    row = lax.axis_index("row")
    col = lax.axis_index("col")
    z, x = row // NX, row % NX
    y, core = col // 2, col % 2

    def ring(yy, cc):
        return (row, yy * 2 + cc)

    def z_peer(d):
        return (lax.rem(z + d, NZ) * NX + x, col)

    def x_peer(d):
        return (z * NX + lax.rem(x + d, NX), col)

    at_root = y == 0
    first = ((core == 1) & (y == 1)) | ((core == 0) & (y == 3))
    last = ((core == 1) & (y == 3)) | ((core == 0) & (y == 1))
    ahead = jnp.where(core == 1, y + 1, y - 1)
    behind = jnp.where(core == 1, y - 1, y + 1)
    lag = jnp.where(first, 3, jnp.where(y == 2, 2, 1))
    mine = 1 - core
    rank = x * NZ + z

    def remote(src, dst, send_sem, recv_sem, device):
        return pltpu.make_async_remote_copy(
            src_ref=src, dst_ref=dst, send_sem=send_sem, recv_sem=recv_sem, device_id=device, device_id_type=MESH
        )

    load_e = pltpu.make_async_copy(e_hbm, e, load_sem.at[0])
    load_v = pltpu.make_async_copy(v_hbm, raw, load_sem.at[1])
    load_f = pltpu.make_async_copy(
        f_hbm.at[0, pl.ds(pl.multiple_of(rank * 8, 8), 8), :], ms.at[1 - core], load_sem.at[2]
    )

    @pl.when(at_root)
    def _():
        load_v.start()
        load_f.start()

    load_e.start()

    barrier = pltpu.get_barrier_semaphore()

    def greet(device):
        pl.semaphore_signal(barrier, inc=1, device_id=device, device_id_type=MESH)

    neighbours = (z_peer(1), z_peer(NZ - 1), x_peer(1), x_peer(NX - 1), ring(y, 1 - core))
    for device in neighbours:
        greet(device)

    @pl.when(y % 2 == 1)
    def _():
        greet(ring(0, 0))
        greet(ring(0, 1))

    @pl.when(jnp.logical_not(at_root | first))
    def _():
        greet(ring(behind, core))

    def transpose_in(ct):
        columns = slice(ct * TILE, (ct + 1) * TILE)
        for start in range(0, ROWS, TILE):
            lanes = slice(start % HALF, start % HALF + TILE)
            vt[1 - core, start // HALF, columns, lanes] = raw[start : start + TILE, columns].T

    @pl.when(at_root)
    def _():
        load_v.wait()
        load_f.wait()
        transpose_in(0)

    pl.semaphore_wait(barrier, len(neighbours) + jnp.where(at_root, 4, jnp.where(last, 0, 1)))

    def tell(n):
        pl.semaphore_signal(known.at[n, 0], inc=1, device_id=z_peer(1), device_id_type=MESH)
        pl.semaphore_signal(known.at[n, 1], inc=1, device_id=z_peer(NZ - 1), device_id_type=MESH)
        if n == 0:
            pl.semaphore_signal(known.at[n, 2], inc=1, device_id=x_peer(1), device_id_type=MESH)

    def hear(n):
        for which in range(3 if n == 0 else 2):
            pl.semaphore_wait(known.at[n, which], 1)

    tell(0)

    def spread(m):
        for device in (ring(0, 1 - core), ring(1, 0), ring(1, 1), ring(3, 0), ring(3, 1)):
            yield remote(ms.at[m], ms.at[m], ms_s.at[m], ms_r.at[m], device)

    def spread_on(m):
        return remote(ms.at[m], ms.at[m], ms_s.at[m], ms_r.at[m], ring(2, core))

    for m in range(2):

        @pl.when(at_root & (core == 1 - m))
        def _():
            for copy in spread(m):
                copy.start()

    def row0(g):
        return pl.multiple_of(jnp.where(g < PER_PANEL, g, GROUPS - 1 - g) * GROUP, GROUP)

    def chunk(k, h):
        g = k // TICKS
        start = pl.multiple_of(row0(g) + (k % TICKS) * TICK, TICK)
        return vt.at[g // PER_PANEL, h, pl.ds(start, TICK), :]

    def piece(k, h, send_sem, device):
        ref = chunk(k, h)
        return remote(ref, ref, send_sem, recv.at[h, k], device)

    def ring_send(k, h):
        return piece(k, h, send.at[h, k], ring(jnp.where(h == 0, 1, 3), jnp.where(h == 0, 1, 0)))

    def direct_send(k, h):
        return piece(k, h, direct.at[h, k - DIRECT], ring(jnp.where(h == 0, 3, 1), jnp.where(h == 0, 1, 0)))

    def relays(k):
        return jnp.logical_not(last | ((y == 2) & (k >= DIRECT)))

    def sib_send(k, h):
        return piece(k, h, sib.at[0], ring(y, 1 - core))

    def ahead_send(k):
        return piece(k, mine, passed.at[k // (CHUNKS // 2)], ring(ahead, core))

    def pass_on(k):
        return piece(k, mine, sib.at[0], ring(y, 1 - core))

    def arrived(k, h):
        piece(k, h, send.at[0, k], ring(y, 1 - core)).wait_recv()

    def ticks(i, begin, end):
        owner = at_root & ((core == 1) == (i < PER_PANEL))
        follower = at_root & ((core == 0) == (i < PER_PANEL))

        for t in range(begin, end):
            k = i * TICKS + t

            @pl.when(owner)
            def _():
                @pl.when(k % (CHUNKS // 2) >= DEPTH)
                def _():
                    for h in range(2):
                        ring_send(k - DEPTH, h).wait_send()

                for h in range(2):
                    ring_send(k, h).start()

                @pl.when(k >= DIRECT)
                def _():
                    for h in range(2):
                        direct_send(k, h).start()

                for h in range(2):
                    sib_send(k, h).start()

            @pl.when(follower)
            def _():
                arrived(k, 0)
                arrived(k, 1)

            @pl.when(jnp.logical_not(at_root))
            def _():
                arrived(k, mine)

                @pl.when(relays(k))
                def _():
                    ahead_send(k).start()

                pass_on(k).start()

    def share(u):
        return 8 if isinstance(u, int) and u >= GROUPS - 1 else 16

    def first_column(u):
        if isinstance(u, int) and u == GROUPS:
            return 32
        return row0(jnp.int32(u) if isinstance(u, int) else u)

    def panel_of(u):
        return 1 if isinstance(u, int) and u >= PER_PANEL else u // PER_PANEL

    def part(ref, u):
        return ref.at[u] if share(u) == 16 else ref.at[u, :, pl.ds(0, 8), :]

    def own(u, position):
        return pl.ds(pl.multiple_of(position * share(u), 8), share(u))

    def to_x(u):
        for d in range(1, NX):
            yield remote(
                wloc.at[u, own(u, lax.rem(x + d, NX)), :],
                x_land.at[u, d - 1, pl.ds(0, share(u)), :], x_s.at[u], x_r.at[u], x_peer(d),
            )

    def to_z(u):
        for d in range(1, NZ):
            ref = zs.at[u, pl.ds(0, share(u)), :]
            yield remote(ref, z_land.at[u, d - 1, pl.ds(0, share(u)), :], z_s.at[u], z_r.at[u], z_peer(d))

    def back_x(u):
        for d in range(1, NX):
            ref = red.at[u, pl.ds(0, share(u)), :]
            yield remote(ref, ag_land.at[u, d - 1, pl.ds(0, share(u)), :], ag_s.at[u], ag_r.at[u], x_peer(d))

    def whole(ref, send_sem, recv_sem):
        return remote(ref, ref, send_sem, recv_sem, ring(y, 1 - core))

    def project(u):
        count = share(u) * NX
        total = jnp.zeros((count, NB), F32)
        for h in range(2):
            high, low = split(vt[panel_of(u), h, pl.ds(first_column(u), count), :])
            both = dot(jnp.concatenate([high, low], axis=0), eh[h * HALF : (h + 1) * HALF, :])
            total += both[:count] + both[count:] + dot(high, el[h * HALF : (h + 1) * HALF, :])
        wloc[u, :count] = total
        for copy in to_x(u):
            copy.start()

    def sum_x(u):
        n = share(u)
        whole(part(x_land, u), x_s.at[u], x_r.at[u]).wait_recv()
        total = wloc[u, own(u, x), :]
        for d in range(NX - 1):
            total += x_land[u, d, :n]
        zs[u, :n] = total
        for copy in to_z(u):
            copy.start()

    def sum_z(u):
        n = share(u)
        whole(part(z_land, u), z_s.at[u], z_r.at[u]).wait_recv()
        total = zs[u, :n]
        for d in range(NZ - 1):
            total += z_land[u, d, :n]
        red[u, :n] = total
        for copy in back_x(u):
            copy.start()

    def gather(u):
        n = share(u)
        whole(part(ag_land, u), ag_s.at[u], ag_r.at[u]).wait_recv()
        base = panel_of(u) * NB + first_column(u)
        wfull[pl.ds(pl.multiple_of(base + x * n, 8), n), :] = red[u, :n]
        for d in range(1, NX):
            origin = lax.rem(x + NX - d, NX)
            wfull[pl.ds(pl.multiple_of(base + origin * n, 8), n), :] = ag_land[u, d - 1, :n]

    def transpose_first(j, h):
        columns = pl.ds(pl.multiple_of(j * TILE, TILE), TILE)
        for start in range(0, HALF, TILE):
            high, low = split(vt[0, h, columns, start : start + TILE].T)
            rows = pl.ds(pl.multiple_of(h * HALF + start, TILE), TILE)
            vn[0, rows, columns] = high
            vn[1, rows, columns] = low

    def transpose_upper(h):
        for start in range(0, HALF, TILE):
            high, low = split(vt[1, h, TILE:, start : start + TILE].T)
            rows = pl.ds(pl.multiple_of(h * HALF + start, TILE), TILE)
            vn[2, rows, :TILE] = high
            vn[2, rows, TILE:] = low

    def transpose_quarter(q):
        for start in range(0, ROWS, TILE):
            lanes = slice(start % HALF, start % HALF + TILE)
            high, low = split(vt[1, start // HALF, q * 64 : (q + 1) * 64, lanes])
            both = jnp.concatenate([high.astype(F32), low.astype(F32)], axis=0).T.astype(BF16)
            vn[3 + q, start : start + TILE, :TILE] = both
            vn[3 + q, start : start + TILE, TILE:] = both

    def m_to_z(m):
        for d in range(1, NZ):
            yield remote(ms.at[m], mz_land.at[m, d - 1], mz_s.at[m], mz_r.at[m], z_peer(d))

    def m_to_x(m):
        for d in range(1, NX):
            yield remote(mz.at[m], mx_land.at[m, d - 1], mx_s.at[m], mx_r.at[m], x_peer(d))

    def m_begin(m):
        is_source = at_root & ((core == 1) if m == 0 else (core == 0))

        @pl.when(jnp.logical_not(is_source | first))
        def _():
            whole(ms.at[m], ms_s.at[m], ms_r.at[m]).wait_recv()

        for copy in m_to_z(m):
            copy.start()

    def m_forward(m):
        whole(ms.at[m], ms_s.at[m], ms_r.at[m]).wait_recv()
        spread_on(m).start()

    def m_middle(m):
        whole(mz_land.at[m], mz_s.at[m], mz_r.at[m]).wait_recv()
        mz[m, pl.ds(pl.multiple_of(z * 8, 8), 8), :] = ms[m]
        for d in range(1, NZ):
            origin = lax.rem(z + NZ - d, NZ)
            mz[m, pl.ds(pl.multiple_of(origin * 8, 8), 8), :] = mz_land[m, d - 1]
        for copy in m_to_x(m):
            copy.start()

    def m_end(m):
        whole(mx_land.at[m], mx_s.at[m], mx_r.at[m]).wait_recv()
        mats[m, pl.ds(pl.multiple_of(x * 64, 64), 64), :] = mz[m]
        for d in range(1, NX):
            origin = lax.rem(x + NX - d, NX)
            mats[m, pl.ds(pl.multiple_of(origin * 64, 64), 64), :] = mx_land[m, d - 1]

    overlap_here = at_root & (core == 0)

    def overlap_to_z():
        for d in range(1, NZ):
            yield remote(gloc.at[lax.rem(z + d, NZ)], gz_land.at[d - 1], gz_s.at[0], gz_r.at[0], z_peer(d))

    def overlap_to_x():
        for d in range(1, NX):
            yield remote(gq.at[lax.rem(x + d, NX)], gx_land.at[d - 1], gx_s.at[0], gx_r.at[0], x_peer(d))

    def overlap_begin():
        total = jnp.zeros((NB, NB), F32)
        for h in range(2):
            ah, al = split(vt[1, h])
            bh, bl = split(vt[0, h])
            total += dot_nt(ah, bh) + dot_nt(ah, bl) + dot_nt(al, bh)
        gacc[...] = total
        for zz in range(NZ):
            for xx in range(NX):
                gloc[zz, xx] = gacc[xx * 64 + zz * 8 : xx * 64 + zz * 8 + 8, :]
        for copy in overlap_to_z():
            copy.start()

    def overlap_middle():
        whole(gz_land, gz_s.at[0], gz_r.at[0]).wait_recv()
        total = gloc[z]
        for d in range(NZ - 1):
            total += gz_land[d]
        gq[...] = total
        for copy in overlap_to_x():
            copy.start()

    def overlap_end():
        whole(gx_land, gx_s.at[0], gx_r.at[0]).wait_recv()
        total = gq[x]
        for d in range(NX - 1):
            total += gx_land[d]
        ms[2] = total
        for copy in spread(2):
            copy.start()

    def split_field():
        load_e.wait()

        def body(n, _):
            rows = pl.ds(pl.multiple_of(n * 256, 256), 256)
            high, low = split(e[rows, :])
            eh[rows, :] = high
            el[rows, :] = low
            return 0

        lax.fori_loop(0, ROWS // 256, body, 0)

    def when(condition, action, *args):
        pl.when(condition)(lambda: action(*args))

    def other_half(done, begin, end):
        @pl.when(jnp.logical_not(at_root))
        def _():
            for t in range(begin, end):
                arrived(done * TICKS + t, core)

    def factors_end():
        m_end(0)
        m_end(1)

    def step(i, _):
        done = i - lag
        when(i < GROUPS, ticks, i, 0, 1)

        @pl.when(i == 0)
        def _():
            when(at_root, transpose_in, 1)

        @pl.when(i == 1)
        def _():
            hear(1)
            tell(2)

        @pl.when(done >= 0)
        def _():
            other_half(done, 0, TICKS)
            project(done)

        when(i < GROUPS, ticks, i, 1, 2)
        when(overlap_here & (i == 4), overlap_begin)
        when(overlap_here & (i == 6), overlap_middle)
        when(overlap_here & (i == 7), overlap_end)
        when(first & (i == 7), m_forward, 2)
        when(i == 7, m_begin, 2)
        when((done >= 1) & (i < GROUPS), sum_x, done - 1)
        when((done >= 3) & (i < GROUPS), sum_z, done - 3)
        when(i < GROUPS, ticks, i, 2, 3)

        @pl.when((i == GROUPS - 1) & last)
        def _():
            other_half(GROUPS - 1, 0, TICKS // 2)
            project(GROUPS - 1)

        when(i == 0, split_field)
        when((done >= 1) & (done <= 4), lambda: transpose_first((done - 1) // 2, (done - 1) % 2))
        when((done == 5) | (done == 6), lambda: transpose_upper(done - 5))
        when(i < GROUPS, ticks, i, 3, 4)

        @pl.when(i == 0)
        def _():
            hear(0)
            tell(1)

        @pl.when(i == 1)
        def _():
            hear(2)

            @pl.when(first)
            def _():
                m_forward(0)
                m_forward(1)


        @pl.when(done == 1)
        def _():
            m_begin(0)
            m_begin(1)

        @pl.when(done == 3)
        def _():
            m_middle(0)
            m_middle(1)

        when(done == 5, factors_end)
        return 0

    lax.fori_loop(0, GROUPS - 1 + lag, step, 0)

    def sums(action, begin, end):
        def body(u, _):
            action(u)
            return 0

        lax.fori_loop(begin, end, body, 0)

    sums(sum_x, GROUPS - 1 - lag, GROUPS - 2)

    @pl.when(jnp.logical_not(last))
    def _():
        other_half(GROUPS - 1, 0, TICKS // 2)
        project(GROUPS - 1)

    other_half(GROUPS - 1, TICKS // 2, TICKS)
    project(GROUPS)

    def left(u):
        whole(part(x_land, u), x_s.at[u], x_r.at[u]).wait_send()
        whole(part(z_land, u), z_s.at[u], z_r.at[u]).wait_send()
        whole(part(ag_land, u), ag_s.at[u], ag_r.at[u]).wait_send()

    def matrices_left():
        for m in range(3):
            whole(mz_land.at[m], mz_s.at[m], mz_r.at[m]).wait_send()
            whole(mx_land.at[m], mx_s.at[m], mx_r.at[m]).wait_send()

            @pl.when(at_root & ((core == 1) if m == 0 else (core == 0)))
            def _():
                whole(mz_land.at[m, pl.ds(0, 5)], ms_s.at[m], ms_r.at[m]).wait_send()

            @pl.when(first)
            def _():
                spread_on(m).wait_send()

        @pl.when(overlap_here)
        def _():
            whole(gz_land, gz_s.at[0], gz_r.at[0]).wait_send()
            whole(gx_land, gx_s.at[0], gx_r.at[0]).wait_send()

    def stream_left():
        @pl.when(jnp.logical_not(at_root))
        def _():
            whole(vt.at[:, mine], sib.at[0], sib.at[0]).wait_send()

            @pl.when(jnp.logical_not(last))
            def _():
                whole(vt.at[0, mine], passed.at[0], sib.at[0]).wait_send()

            @pl.when(first)
            def _():
                whole(vt.at[1, mine], passed.at[1], sib.at[0]).wait_send()

            @pl.when(y == 2)
            def _():
                sent = NB - (CHUNKS - DIRECT) * TICK
                whole(vt.at[1, mine, pl.ds(0, sent), :], passed.at[1], sib.at[0]).wait_send()

        @pl.when(at_root)
        def _():
            whole(vt.at[1 - core], sib.at[0], sib.at[0]).wait_send()
            base = (1 - core) * (CHUNKS // 2)
            for h in range(2):
                for t in range(CHUNKS // 2 - DEPTH, CHUNKS // 2):
                    ring_send(base + t, h).wait_send()

        @pl.when(at_root & (core == 0))
        def _():
            for h in range(2):
                for k in range(DIRECT, CHUNKS):
                    direct_send(k, h).wait_send()

    def quarter(q, value):
        high, low = split(value)
        stacked = jnp.concatenate([high, high, low, jnp.zeros_like(low)], axis=0)
        return dot(vn[3 + q], stacked)

    sums(sum_z, GROUPS - 3 - lag, GROUPS - 4)
    sum_x(6)
    sum_z(4)
    m_middle(2)
    for u in range(4):
        gather(u)
    first_s = product(mats[0], wfull[:NB, :])
    high, low = split(first_s)
    e[...] -= dot(vn[0], high) + dot(vn[0], low) + dot(vn[1], high)
    sum_x(7)
    transpose_quarter(1)
    sum_x(8)
    transpose_quarter(0)
    sum_z(5)
    stream_left()
    gather(4)
    m_end(2)
    correction = product(mats[2], first_s)
    sum_z(6)
    gather(5)
    upper = wfull[NB + TILE :, :] - correction[TILE:]
    high, low = split(product(mats[1, TILE:, TILE:], upper))
    sum_z(7)
    sum_z(8)
    e[...] -= dot(vn[2], jnp.concatenate([high, high], axis=0)) + dot(vn[2, :, :TILE], low)
    gather(6)
    next_u = wfull[NB + 64 : NB + TILE, :] - correction[64:TILE]
    known_u = jnp.concatenate([jnp.zeros_like(next_u), next_u, upper], axis=0)
    e[...] -= quarter(1, product(mats[1, 64:TILE, :], known_u))
    matrices_left()
    for u in range(UNITS):
        left(u)
    gather(7)
    gather(8)
    last_u = wfull[NB : NB + 64, :] - correction[:64]
    out[...] = e[...] - quarter(0, product(mats[1, :64, :], jnp.concatenate([last_u, next_u, upper], axis=0)))


def local(eigvecs, reflectors, factors):
    vmem, dma = pltpu.VMEM, pltpu.SemaphoreType.DMA
    return pl.pallas_call(
        kernel,
        out_shape=jax.ShapeDtypeStruct((ROWS, NB), F32),
        in_specs=[pl.BlockSpec(memory_space=pltpu.HBM)] * 3,
        out_specs=pl.BlockSpec(memory_space=pltpu.VMEM),
        scratch_shapes=[
            vmem((ROWS, NB), F32),
            vmem((ROWS, NB), F32),
            vmem((ROWS, NB), BF16),
            vmem((ROWS, NB), BF16),
            vmem((2, 2, NB, HALF), F32),
            vmem((5, ROWS, NB), BF16),
            vmem((UNITS, GROUP, NB), F32),
            vmem((UNITS, NX - 1, 16, NB), F32),
            vmem((UNITS, 16, NB), F32),
            vmem((UNITS, NZ - 1, 16, NB), F32),
            vmem((UNITS, 16, NB), F32),
            vmem((UNITS, NX - 1, 16, NB), F32),
            vmem((2 * NB, NB), F32),
            vmem((3, 8, NB), F32),
            vmem((3, NZ - 1, 8, NB), F32),
            vmem((3, 64, NB), F32),
            vmem((3, NX - 1, 64, NB), F32),
            vmem((3, NB, NB), F32),
            vmem((NB, NB), F32),
            vmem((NZ, NX, 8, NB), F32),
            vmem((NZ - 1, NX, 8, NB), F32),
            vmem((NX, 8, NB), F32),
            vmem((NX - 1, 8, NB), F32),
            pltpu.SemaphoreType.REGULAR((3, 3)),
            dma((3,)),
            dma((2, CHUNKS)),
            dma((2, CHUNKS)),
            dma((1,)),
            dma((2,)),
            dma((2, CHUNKS - DIRECT)),
            *[dma((UNITS,))] * 6,
            *[dma((3,))] * 6,
            *[dma((1,))] * 4,
        ],
        compiler_params=pltpu.CompilerParams(collective_id=0, has_side_effects=True, vmem_limit_bytes=50 * 2**20),
    )(eigvecs, reflectors, factors)


def solution(mesh):
    in_specs = (P("row", "col"), P("row", "col"), P("col", None, None))
    return jax.shard_map(local, mesh=mesh, in_specs=in_specs, out_specs=P("row", "col"), check_vma=False)
```

```python
import jax
import jax.numpy as jnp
from jax import lax
from jax.experimental import pallas as pl
from jax.experimental.pallas import tpu as pltpu
from jax.sharding import PartitionSpec as P

MESH = pl.DeviceIdType.MESH
F32, BF16 = jnp.float32, jnp.bfloat16
NZ, NX, NCOL = 8, 4, 8
NB = 256
ROWS = 3072
HALF = ROWS // 2
TICK = 16
GROUP = 64
TICKS = GROUP // TICK
PER_PANEL = NB // GROUP
GROUPS = 2 * PER_PANEL
CHUNKS = GROUPS * TICKS
TILE = 128
DEPTH = 3
DIRECT = CHUNKS - 4
UNITS = GROUPS + 1


def split(value):
    high = value.astype(BF16)
    return high, (value - high.astype(F32)).astype(BF16)


def dot(left, right):
    return jnp.dot(left, right, preferred_element_type=F32)


def dot_nt(left, right):
    return lax.dot_general(left, right, (((1,), (1,)), ((), ())), preferred_element_type=F32)


def product(left, right):
    lh, ll = split(left)
    rh, rl = split(right)
    return dot(lh, rh) + dot(lh, rl) + dot(ll, rh)


def kernel(
    e_hbm, v_hbm, f_hbm, out,
    e, raw, eh, el, vt, vn,
    wloc, x_land, zs, z_land, red, ag_land, wfull,
    ms, mz_land, mz, mx_land, mats,
    gacc, gloc, gz_land, gq, gx_land,
    known, load_sem, recv, send, sib, passed,
    direct, x_s, x_r, z_s, z_r, ag_s, ag_r,
    ms_s, ms_r, mz_s, mz_r, mx_s, mx_r,
    gz_s, gz_r, gx_s, gx_r,
):
    row = lax.axis_index("row")
    col = lax.axis_index("col")
    z, x = row // NX, row % NX
    y, core = col // 2, col % 2

    def ring(yy, cc):
        return (row, yy * 2 + cc)

    def z_peer(d):
        return (lax.rem(z + d, NZ) * NX + x, col)

    def x_peer(d):
        return (z * NX + lax.rem(x + d, NX), col)

    at_root = y == 0
    side = jnp.where(y == 3, 1 - core, core)
    first = (core == 1) & (y % 2 == 1)
    last = (core == 0) & (y % 2 == 1)
    ahead = (jnp.where(side == 1, y + 1, y - 1), jnp.where(y == 1, core, 0))
    behind = (jnp.where(side == 1, y - 1, y + 1), jnp.where(y == 1, 0, 1))
    lag = jnp.where(first, 3, 1)
    mine = 1 - side
    rank = x * NZ + z

    def remote(src, dst, send_sem, recv_sem, device):
        return pltpu.make_async_remote_copy(
            src_ref=src, dst_ref=dst, send_sem=send_sem, recv_sem=recv_sem, device_id=device, device_id_type=MESH
        )

    load_e = pltpu.make_async_copy(e_hbm, e, load_sem.at[0])
    load_v = pltpu.make_async_copy(v_hbm, raw, load_sem.at[1])
    load_f = pltpu.make_async_copy(
        f_hbm.at[0, pl.ds(pl.multiple_of(rank * 8, 8), 8), :], ms.at[1 - core], load_sem.at[2]
    )

    @pl.when(at_root)
    def _():
        load_v.start()
        load_f.start()

    load_e.start()

    barrier = pltpu.get_barrier_semaphore()

    def greet(device):
        pl.semaphore_signal(barrier, inc=1, device_id=device, device_id_type=MESH)

    neighbours = (z_peer(1), z_peer(NZ - 1), x_peer(1), x_peer(NX - 1), ring(y, 1 - core))
    for device in neighbours:
        greet(device)

    @pl.when(y % 2 == 1)
    def _():
        greet(ring(0, 0))
        greet(ring(0, 1))

    @pl.when(jnp.logical_not(at_root | first))
    def _():
        greet(ring(*behind))

    def transpose_in(ct):
        columns = slice(ct * TILE, (ct + 1) * TILE)
        for start in range(0, ROWS, TILE):
            lanes = slice(start % HALF, start % HALF + TILE)
            vt[1 - core, start // HALF, columns, lanes] = raw[start : start + TILE, columns].T

    @pl.when(at_root)
    def _():
        load_v.wait()
        load_f.wait()
        transpose_in(0)

    pl.semaphore_wait(barrier, len(neighbours) + jnp.where(at_root, 4, jnp.where(last, 0, 1)))

    def tell(n):
        pl.semaphore_signal(known.at[n, 0], inc=1, device_id=z_peer(1), device_id_type=MESH)
        pl.semaphore_signal(known.at[n, 1], inc=1, device_id=z_peer(NZ - 1), device_id_type=MESH)
        if n == 0:
            pl.semaphore_signal(known.at[n, 2], inc=1, device_id=x_peer(1), device_id_type=MESH)

    def hear(n):
        for which in range(3 if n == 0 else 2):
            pl.semaphore_wait(known.at[n, which], 1)

    tell(0)

    def spread(m):
        for device in (ring(0, 1 - core), ring(1, 0), ring(1, 1), ring(3, 0), ring(3, 1)):
            yield remote(ms.at[m], ms.at[m], ms_s.at[m], ms_r.at[m], device)

    def spread_on(m):
        return remote(ms.at[m], ms.at[m], ms_s.at[m], ms_r.at[m], ring(*ahead))

    for m in range(2):

        @pl.when(at_root & (core == 1 - m))
        def _():
            for copy in spread(m):
                copy.start()

    def row0(g):
        return pl.multiple_of(jnp.where(g < PER_PANEL, g, GROUPS - 1 - g) * GROUP, GROUP)

    def chunk(k, h):
        g = k // TICKS
        start = pl.multiple_of(row0(g) + (k % TICKS) * TICK, TICK)
        return vt.at[g // PER_PANEL, h, pl.ds(start, TICK), :]

    def piece(k, h, send_sem, device):
        ref = chunk(k, h)
        return remote(ref, ref, send_sem, recv.at[h, k], device)

    def ring_send(k, h):
        return piece(k, h, send.at[h, k], ring(jnp.where(h == 0, 1, 3), 1))

    def direct_send(k, h):
        return piece(k, h, direct.at[h, k - DIRECT], ring(jnp.where(h == 0, 3, 1), 0))

    def relays(k):
        return jnp.logical_not(last | ((y == 2) & (k >= DIRECT)))

    def sib_send(k, h):
        return piece(k, h, sib.at[0], ring(y, 1 - core))

    def ahead_send(k):
        return piece(k, mine, passed.at[k // (CHUNKS // 2)], ring(*ahead))

    def pass_on(k):
        return piece(k, mine, sib.at[0], ring(y, 1 - core))

    def arrived(k, h):
        piece(k, h, send.at[0, k], ring(y, 1 - core)).wait_recv()

    def ticks(i, begin, end):
        owner = at_root & ((core == 1) == (i < PER_PANEL))
        follower = at_root & ((core == 0) == (i < PER_PANEL))

        for t in range(begin, end):
            k = i * TICKS + t

            @pl.when(owner)
            def _():
                @pl.when(k % (CHUNKS // 2) >= DEPTH)
                def _():
                    for h in range(2):
                        ring_send(k - DEPTH, h).wait_send()

                for h in range(2):
                    ring_send(k, h).start()

                @pl.when(k >= DIRECT)
                def _():
                    for h in range(2):
                        direct_send(k, h).start()

                for h in range(2):
                    sib_send(k, h).start()

            @pl.when(follower)
            def _():
                arrived(k, 0)
                arrived(k, 1)

            @pl.when(jnp.logical_not(at_root))
            def _():
                arrived(k, mine)

                @pl.when(relays(k))
                def _():
                    ahead_send(k).start()

                pass_on(k).start()

    def share(u):
        return 8 if isinstance(u, int) and u >= GROUPS - 1 else 16

    def first_column(u):
        if isinstance(u, int) and u == GROUPS:
            return 32
        return row0(jnp.int32(u) if isinstance(u, int) else u)

    def panel_of(u):
        return 1 if isinstance(u, int) and u >= PER_PANEL else u // PER_PANEL

    def part(ref, u):
        return ref.at[u] if share(u) == 16 else ref.at[u, :, pl.ds(0, 8), :]

    def own(u, position):
        return pl.ds(pl.multiple_of(position * share(u), 8), share(u))

    def to_x(u):
        for d in range(1, NX):
            yield remote(
                wloc.at[u, own(u, lax.rem(x + d, NX)), :],
                x_land.at[u, d - 1, pl.ds(0, share(u)), :], x_s.at[u], x_r.at[u], x_peer(d),
            )

    def to_z(u):
        for d in range(1, NZ):
            ref = zs.at[u, pl.ds(0, share(u)), :]
            yield remote(ref, z_land.at[u, d - 1, pl.ds(0, share(u)), :], z_s.at[u], z_r.at[u], z_peer(d))

    def back_x(u):
        for d in range(1, NX):
            ref = red.at[u, pl.ds(0, share(u)), :]
            yield remote(ref, ag_land.at[u, d - 1, pl.ds(0, share(u)), :], ag_s.at[u], ag_r.at[u], x_peer(d))

    def whole(ref, send_sem, recv_sem):
        return remote(ref, ref, send_sem, recv_sem, ring(y, 1 - core))

    def project(u):
        count = share(u) * NX
        total = jnp.zeros((count, NB), F32)
        for h in range(2):
            high, low = split(vt[panel_of(u), h, pl.ds(first_column(u), count), :])
            both = dot(jnp.concatenate([high, low], axis=0), eh[h * HALF : (h + 1) * HALF, :])
            total += both[:count] + both[count:] + dot(high, el[h * HALF : (h + 1) * HALF, :])
        wloc[u, :count] = total
        for copy in to_x(u):
            copy.start()

    def sum_x(u):
        n = share(u)
        whole(part(x_land, u), x_s.at[u], x_r.at[u]).wait_recv()
        total = wloc[u, own(u, x), :]
        for d in range(NX - 1):
            total += x_land[u, d, :n]
        zs[u, :n] = total
        for copy in to_z(u):
            copy.start()

    def sum_z(u):
        n = share(u)
        whole(part(z_land, u), z_s.at[u], z_r.at[u]).wait_recv()
        total = zs[u, :n]
        for d in range(NZ - 1):
            total += z_land[u, d, :n]
        red[u, :n] = total
        for copy in back_x(u):
            copy.start()

    def gather(u):
        n = share(u)
        whole(part(ag_land, u), ag_s.at[u], ag_r.at[u]).wait_recv()
        base = panel_of(u) * NB + first_column(u)
        wfull[pl.ds(pl.multiple_of(base + x * n, 8), n), :] = red[u, :n]
        for d in range(1, NX):
            origin = lax.rem(x + NX - d, NX)
            wfull[pl.ds(pl.multiple_of(base + origin * n, 8), n), :] = ag_land[u, d - 1, :n]

    def transpose_first(j, h):
        columns = pl.ds(pl.multiple_of(j * TILE, TILE), TILE)
        for start in range(0, HALF, TILE):
            high, low = split(vt[0, h, columns, start : start + TILE].T)
            rows = pl.ds(pl.multiple_of(h * HALF + start, TILE), TILE)
            vn[0, rows, columns] = high
            vn[1, rows, columns] = low

    def transpose_upper(h):
        for start in range(0, HALF, TILE):
            high, low = split(vt[1, h, TILE:, start : start + TILE].T)
            rows = pl.ds(pl.multiple_of(h * HALF + start, TILE), TILE)
            vn[2, rows, :TILE] = high
            vn[2, rows, TILE:] = low

    def transpose_quarter(q):
        for start in range(0, ROWS, TILE):
            lanes = slice(start % HALF, start % HALF + TILE)
            high, low = split(vt[1, start // HALF, q * 64 : (q + 1) * 64, lanes])
            both = jnp.concatenate([high.astype(F32), low.astype(F32)], axis=0).T.astype(BF16)
            vn[3 + q, start : start + TILE, :TILE] = both
            vn[3 + q, start : start + TILE, TILE:] = both

    def m_to_z(m):
        for d in range(1, NZ):
            yield remote(ms.at[m], mz_land.at[m, d - 1], mz_s.at[m], mz_r.at[m], z_peer(d))

    def m_to_x(m):
        for d in range(1, NX):
            yield remote(mz.at[m], mx_land.at[m, d - 1], mx_s.at[m], mx_r.at[m], x_peer(d))

    def m_begin(m):
        is_source = at_root & ((core == 1) if m == 0 else (core == 0))

        @pl.when(jnp.logical_not(is_source | first))
        def _():
            whole(ms.at[m], ms_s.at[m], ms_r.at[m]).wait_recv()

        for copy in m_to_z(m):
            copy.start()

    def m_forward(m):
        whole(ms.at[m], ms_s.at[m], ms_r.at[m]).wait_recv()
        spread_on(m).start()

    def m_middle(m):
        whole(mz_land.at[m], mz_s.at[m], mz_r.at[m]).wait_recv()
        mz[m, pl.ds(pl.multiple_of(z * 8, 8), 8), :] = ms[m]
        for d in range(1, NZ):
            origin = lax.rem(z + NZ - d, NZ)
            mz[m, pl.ds(pl.multiple_of(origin * 8, 8), 8), :] = mz_land[m, d - 1]
        for copy in m_to_x(m):
            copy.start()

    def m_end(m):
        whole(mx_land.at[m], mx_s.at[m], mx_r.at[m]).wait_recv()
        mats[m, pl.ds(pl.multiple_of(x * 64, 64), 64), :] = mz[m]
        for d in range(1, NX):
            origin = lax.rem(x + NX - d, NX)
            mats[m, pl.ds(pl.multiple_of(origin * 64, 64), 64), :] = mx_land[m, d - 1]

    overlap_here = at_root & (core == 0)

    def overlap_to_z():
        for d in range(1, NZ):
            yield remote(gloc.at[lax.rem(z + d, NZ)], gz_land.at[d - 1], gz_s.at[0], gz_r.at[0], z_peer(d))

    def overlap_to_x():
        for d in range(1, NX):
            yield remote(gq.at[lax.rem(x + d, NX)], gx_land.at[d - 1], gx_s.at[0], gx_r.at[0], x_peer(d))

    def overlap_begin():
        total = jnp.zeros((NB, NB), F32)
        for h in range(2):
            ah, al = split(vt[1, h])
            bh, bl = split(vt[0, h])
            total += dot_nt(ah, bh) + dot_nt(ah, bl) + dot_nt(al, bh)
        gacc[...] = total
        for zz in range(NZ):
            for xx in range(NX):
                gloc[zz, xx] = gacc[xx * 64 + zz * 8 : xx * 64 + zz * 8 + 8, :]
        for copy in overlap_to_z():
            copy.start()

    def overlap_middle():
        whole(gz_land, gz_s.at[0], gz_r.at[0]).wait_recv()
        total = gloc[z]
        for d in range(NZ - 1):
            total += gz_land[d]
        gq[...] = total
        for copy in overlap_to_x():
            copy.start()

    def overlap_end():
        whole(gx_land, gx_s.at[0], gx_r.at[0]).wait_recv()
        total = gq[x]
        for d in range(NX - 1):
            total += gx_land[d]
        ms[2] = total
        for copy in spread(2):
            copy.start()

    def split_field():
        load_e.wait()

        def body(n, _):
            rows = pl.ds(pl.multiple_of(n * 256, 256), 256)
            high, low = split(e[rows, :])
            eh[rows, :] = high
            el[rows, :] = low
            return 0

        lax.fori_loop(0, ROWS // 256, body, 0)

    def when(condition, action, *args):
        pl.when(condition)(lambda: action(*args))

    def other_half(done, begin, end):
        @pl.when(jnp.logical_not(at_root))
        def _():
            for t in range(begin, end):
                arrived(done * TICKS + t, 1 - mine)

    def factors_end():
        m_end(0)
        m_end(1)

    def step(i, _):
        done = i - lag
        when(i < GROUPS, ticks, i, 0, 1)

        @pl.when(i == 0)
        def _():
            when(at_root, transpose_in, 1)

        @pl.when(i == 1)
        def _():
            hear(1)
            tell(2)

        @pl.when(done >= 0)
        def _():
            other_half(done, 0, TICKS)
            project(done)

        when(i < GROUPS, ticks, i, 1, 2)
        when(overlap_here & (i == 4), overlap_begin)
        when(overlap_here & (i == 6), overlap_middle)
        when(overlap_here & (i == 7), overlap_end)
        when(first & (i == 7), m_forward, 2)
        when(i == 7, m_begin, 2)
        when((done >= 1) & (i <= GROUPS), sum_x, done - 1)
        when((done >= 3) & (i <= GROUPS), sum_z, done - 3)
        when(i < GROUPS, ticks, i, 2, 3)

        @pl.when((i == GROUPS - 1) & last)
        def _():
            other_half(GROUPS - 1, 0, TICKS // 2)
            project(GROUPS - 1)

        when(i == 0, split_field)
        when((done >= 1) & (done <= 4), lambda: transpose_first((done - 1) // 2, (done - 1) % 2))
        when((done == 5) | (done == 6), lambda: transpose_upper(done - 5))
        when(i < GROUPS, ticks, i, 3, 4)

        @pl.when(i == 0)
        def _():
            hear(0)
            tell(1)

        @pl.when(i == 1)
        def _():
            hear(2)

            @pl.when(first)
            def _():
                m_forward(0)
                m_forward(1)


        @pl.when(done == 1)
        def _():
            m_begin(0)
            m_begin(1)

        @pl.when(done == 3)
        def _():
            m_middle(0)
            m_middle(1)

        when(done == 5, factors_end)
        return 0

    lax.fori_loop(0, GROUPS - 1 + lag, step, 0)

    def sums(action, begin, end):
        def body(u, _):
            action(u)
            return 0

        lax.fori_loop(begin, end, body, 0)

    caught_up = jnp.where(first, 1, 0)
    sums(sum_x, GROUPS - 1 - lag + caught_up, GROUPS - 2)

    @pl.when(jnp.logical_not(last))
    def _():
        other_half(GROUPS - 1, 0, TICKS // 2)
        project(GROUPS - 1)

    other_half(GROUPS - 1, TICKS // 2, TICKS)
    project(GROUPS)

    def left(u):
        whole(part(x_land, u), x_s.at[u], x_r.at[u]).wait_send()
        whole(part(z_land, u), z_s.at[u], z_r.at[u]).wait_send()
        whole(part(ag_land, u), ag_s.at[u], ag_r.at[u]).wait_send()

    def matrices_left():
        for m in range(3):
            whole(mz_land.at[m], mz_s.at[m], mz_r.at[m]).wait_send()
            whole(mx_land.at[m], mx_s.at[m], mx_r.at[m]).wait_send()

            @pl.when(at_root & ((core == 1) if m == 0 else (core == 0)))
            def _():
                whole(mz_land.at[m, pl.ds(0, 5)], ms_s.at[m], ms_r.at[m]).wait_send()

            @pl.when(first)
            def _():
                spread_on(m).wait_send()

        @pl.when(overlap_here)
        def _():
            whole(gz_land, gz_s.at[0], gz_r.at[0]).wait_send()
            whole(gx_land, gx_s.at[0], gx_r.at[0]).wait_send()

    def stream_left():
        @pl.when(jnp.logical_not(at_root))
        def _():
            whole(vt.at[:, mine], sib.at[0], sib.at[0]).wait_send()

            @pl.when(jnp.logical_not(last))
            def _():
                whole(vt.at[0, mine], passed.at[0], sib.at[0]).wait_send()

            @pl.when(first)
            def _():
                whole(vt.at[1, mine], passed.at[1], sib.at[0]).wait_send()

            @pl.when(y == 2)
            def _():
                sent = NB - (CHUNKS - DIRECT) * TICK
                whole(vt.at[1, mine, pl.ds(0, sent), :], passed.at[1], sib.at[0]).wait_send()

        @pl.when(at_root)
        def _():
            whole(vt.at[1 - core], sib.at[0], sib.at[0]).wait_send()
            base = (1 - core) * (CHUNKS // 2)
            for h in range(2):
                for t in range(CHUNKS // 2 - DEPTH, CHUNKS // 2):
                    ring_send(base + t, h).wait_send()

        @pl.when(at_root & (core == 0))
        def _():
            for h in range(2):
                for k in range(DIRECT, CHUNKS):
                    direct_send(k, h).wait_send()

    def quarter(q, value):
        high, low = split(value)
        stacked = jnp.concatenate([high, high, low, jnp.zeros_like(low)], axis=0)
        return dot(vn[3 + q], stacked)

    sums(sum_z, GROUPS - 3 - lag + caught_up, GROUPS - 4)
    sum_x(6)
    sum_z(4)
    m_middle(2)
    for u in range(4):
        gather(u)
    first_s = product(mats[0], wfull[:NB, :])
    high, low = split(first_s)
    e[...] -= dot(vn[0], high) + dot(vn[0], low) + dot(vn[1], high)
    sum_x(7)
    transpose_quarter(1)
    sum_x(8)
    transpose_quarter(0)
    sum_z(5)
    stream_left()
    gather(4)
    m_end(2)
    correction = product(mats[2], first_s)
    sum_z(6)
    gather(5)
    upper = wfull[NB + TILE :, :] - correction[TILE:]
    high, low = split(product(mats[1, TILE:, TILE:], upper))
    sum_z(7)
    sum_z(8)
    e[...] -= dot(vn[2], jnp.concatenate([high, high], axis=0)) + dot(vn[2, :, :TILE], low)
    gather(6)
    next_u = wfull[NB + 64 : NB + TILE, :] - correction[64:TILE]
    known_u = jnp.concatenate([jnp.zeros_like(next_u), next_u, upper], axis=0)
    e[...] -= quarter(1, product(mats[1, 64:TILE, :], known_u))
    matrices_left()
    for u in range(UNITS):
        left(u)
    gather(7)
    gather(8)
    last_u = wfull[NB : NB + 64, :] - correction[:64]
    out[...] = e[...] - quarter(0, product(mats[1, :64, :], jnp.concatenate([last_u, next_u, upper], axis=0)))


def local(eigvecs, reflectors, factors):
    vmem, dma = pltpu.VMEM, pltpu.SemaphoreType.DMA
    return pl.pallas_call(
        kernel,
        out_shape=jax.ShapeDtypeStruct((ROWS, NB), F32),
        in_specs=[pl.BlockSpec(memory_space=pltpu.HBM)] * 3,
        out_specs=pl.BlockSpec(memory_space=pltpu.VMEM),
        scratch_shapes=[
            vmem((ROWS, NB), F32),
            vmem((ROWS, NB), F32),
            vmem((ROWS, NB), BF16),
            vmem((ROWS, NB), BF16),
            vmem((2, 2, NB, HALF), F32),
            vmem((5, ROWS, NB), BF16),
            vmem((UNITS, GROUP, NB), F32),
            vmem((UNITS, NX - 1, 16, NB), F32),
            vmem((UNITS, 16, NB), F32),
            vmem((UNITS, NZ - 1, 16, NB), F32),
            vmem((UNITS, 16, NB), F32),
            vmem((UNITS, NX - 1, 16, NB), F32),
            vmem((2 * NB, NB), F32),
            vmem((3, 8, NB), F32),
            vmem((3, NZ - 1, 8, NB), F32),
            vmem((3, 64, NB), F32),
            vmem((3, NX - 1, 64, NB), F32),
            vmem((3, NB, NB), F32),
            vmem((NB, NB), F32),
            vmem((NZ, NX, 8, NB), F32),
            vmem((NZ - 1, NX, 8, NB), F32),
            vmem((NX, 8, NB), F32),
            vmem((NX - 1, 8, NB), F32),
            pltpu.SemaphoreType.REGULAR((3, 3)),
            dma((3,)),
            dma((2, CHUNKS)),
            dma((2, CHUNKS)),
            dma((1,)),
            dma((2,)),
            dma((2, CHUNKS - DIRECT)),
            *[dma((UNITS,))] * 6,
            *[dma((3,))] * 6,
            *[dma((1,))] * 4,
        ],
        compiler_params=pltpu.CompilerParams(collective_id=0, has_side_effects=True, vmem_limit_bytes=50 * 2**20),
    )(eigvecs, reflectors, factors)


def solution(mesh):
    in_specs = (P("row", "col"), P("row", "col"), P("col", None, None))
    return jax.shard_map(local, mesh=mesh, in_specs=in_specs, out_specs=P("row", "col"), check_vma=False)
```

```python
import jax
import jax.numpy as jnp
from jax import lax
from jax.experimental import pallas as pl
from jax.experimental.pallas import tpu as pltpu
from jax.sharding import PartitionSpec as P

MESH = pl.DeviceIdType.MESH
F32, BF16 = jnp.float32, jnp.bfloat16
NZ, NX, NCOL = 8, 4, 8
NB = 256
ROWS = 3072
HALF = ROWS // 2
TICK = 16
GROUP = 64
TICKS = GROUP // TICK
PER_PANEL = NB // GROUP
GROUPS = 2 * PER_PANEL
CHUNKS = GROUPS * TICKS
TILE = 128
DEPTH = 3
DIRECT = CHUNKS - 4
UNITS = GROUPS + 1


def split(value):
    high = value.astype(BF16)
    return high, (value - high.astype(F32)).astype(BF16)


def dot(left, right):
    return jnp.dot(left, right, preferred_element_type=F32)


def dot_nt(left, right):
    return lax.dot_general(left, right, (((1,), (1,)), ((), ())), preferred_element_type=F32)


def product(left, right):
    lh, ll = split(left)
    rh, rl = split(right)
    return dot(lh, rh) + dot(lh, rl) + dot(ll, rh)


def kernel(
    e_hbm, v_hbm, f_hbm, out,
    e, raw, eh, el, vt, vn,
    wloc, x_land, zs, z_land, red, ag_land, wfull,
    ms, mz_land, mz, mx_land, mats,
    gacc, gloc, gz_land, gq, gx_land,
    known, load_sem, recv, send, sib, passed,
    direct, x_s, x_r, z_s, z_r, ag_s, ag_r,
    ms_s, ms_r, mz_s, mz_r, mx_s, mx_r,
    gz_s, gz_r, gx_s, gx_r,
):
    row = lax.axis_index("row")
    col = lax.axis_index("col")
    z, x = row // NX, row % NX
    y, core = col // 2, col % 2

    def ring(yy, cc):
        return (row, yy * 2 + cc)

    def z_peer(d):
        return (lax.rem(z + d, NZ) * NX + x, col)

    def x_peer(d):
        return (z * NX + lax.rem(x + d, NX), col)

    at_root = y == 0
    side = jnp.where(y == 3, 1 - core, core)
    first = (core == 1) & (y % 2 == 1)
    last = (core == 0) & (y % 2 == 1)
    ahead = (jnp.where(side == 1, y + 1, y - 1), jnp.where(y == 1, core, 0))
    behind = (jnp.where(side == 1, y - 1, y + 1), jnp.where(y == 1, 0, 1))
    lag = jnp.where(first, 3, 1)
    mine = 1 - side
    rank = x * NZ + z

    def remote(src, dst, send_sem, recv_sem, device):
        return pltpu.make_async_remote_copy(
            src_ref=src, dst_ref=dst, send_sem=send_sem, recv_sem=recv_sem, device_id=device, device_id_type=MESH
        )

    load_e = pltpu.make_async_copy(e_hbm, e, load_sem.at[0])
    load_v = pltpu.make_async_copy(v_hbm, raw, load_sem.at[1])
    load_f = pltpu.make_async_copy(
        f_hbm.at[0, pl.ds(pl.multiple_of(rank * 8, 8), 8), :], ms.at[1 - core], load_sem.at[2]
    )

    @pl.when(at_root)
    def _():
        load_v.start()
        load_f.start()

    load_e.start()

    barrier = pltpu.get_barrier_semaphore()

    def greet(device):
        pl.semaphore_signal(barrier, inc=1, device_id=device, device_id_type=MESH)

    neighbours = (z_peer(1), z_peer(NZ - 1), x_peer(1), x_peer(NX - 1), ring(y, 1 - core))
    for device in neighbours:
        greet(device)

    @pl.when(y % 2 == 1)
    def _():
        greet(ring(0, 0))
        greet(ring(0, 1))

    @pl.when(jnp.logical_not(at_root | first))
    def _():
        greet(ring(*behind))

    def transpose_in(ct):
        columns = slice(ct * TILE, (ct + 1) * TILE)
        for start in range(0, ROWS, TILE):
            lanes = slice(start % HALF, start % HALF + TILE)
            vt[1 - core, start // HALF, columns, lanes] = raw[start : start + TILE, columns].T

    @pl.when(at_root)
    def _():
        load_v.wait()
        load_f.wait()
        transpose_in(0)

    pl.semaphore_wait(barrier, len(neighbours) + jnp.where(at_root, 4, jnp.where(last, 0, 1)))

    def tell(n):
        pl.semaphore_signal(known.at[n, 0], inc=1, device_id=z_peer(1), device_id_type=MESH)
        pl.semaphore_signal(known.at[n, 1], inc=1, device_id=z_peer(NZ - 1), device_id_type=MESH)
        if n == 0:
            pl.semaphore_signal(known.at[n, 2], inc=1, device_id=x_peer(1), device_id_type=MESH)

    def hear(n):
        for which in range(3 if n == 0 else 2):
            pl.semaphore_wait(known.at[n, which], 1)

    tell(0)

    def spread(m):
        for device in (ring(0, 1 - core), ring(1, 0), ring(1, 1), ring(3, 0), ring(3, 1)):
            yield remote(ms.at[m], ms.at[m], ms_s.at[m], ms_r.at[m], device)

    def spread_on(m):
        return remote(ms.at[m], ms.at[m], ms_s.at[m], ms_r.at[m], ring(*ahead))

    for m in range(2):

        @pl.when(at_root & (core == 1 - m))
        def _():
            for copy in spread(m):
                copy.start()

    def row0(g):
        return pl.multiple_of(jnp.where(g < PER_PANEL, g, GROUPS - 1 - g) * GROUP, GROUP)

    def chunk(k, h):
        g = k // TICKS
        start = pl.multiple_of(row0(g) + (k % TICKS) * TICK, TICK)
        return vt.at[g // PER_PANEL, h, pl.ds(start, TICK), :]

    def piece(k, h, send_sem, device):
        ref = chunk(k, h)
        return remote(ref, ref, send_sem, recv.at[h, k], device)

    def ring_send(k, h):
        return piece(k, h, send.at[h, k], ring(jnp.where(h == 0, 1, 3), 1))

    def direct_send(k, h):
        return piece(k, h, direct.at[h, k - DIRECT], ring(jnp.where(h == 0, 3, 1), 0))

    def relays(k):
        return jnp.logical_not(last | ((y == 2) & (k >= DIRECT)))

    def sib_send(k, h):
        return piece(k, h, sib.at[0], ring(y, 1 - core))

    def ahead_send(k):
        return piece(k, mine, passed.at[k // (CHUNKS // 2)], ring(*ahead))

    def pass_on(k):
        return piece(k, mine, sib.at[0], ring(y, 1 - core))

    def arrived(k, h):
        piece(k, h, send.at[0, k], ring(y, 1 - core)).wait_recv()

    def ticks(i, begin, end):
        owner = at_root & ((core == 1) == (i < PER_PANEL))
        follower = at_root & ((core == 0) == (i < PER_PANEL))

        for t in range(begin, end):
            k = i * TICKS + t

            @pl.when(owner)
            def _():
                @pl.when(k % (CHUNKS // 2) >= DEPTH)
                def _():
                    for h in range(2):
                        ring_send(k - DEPTH, h).wait_send()

                for h in range(2):
                    ring_send(k, h).start()

                @pl.when(k >= DIRECT)
                def _():
                    for h in range(2):
                        direct_send(k, h).start()

                for h in range(2):
                    sib_send(k, h).start()

            @pl.when(follower)
            def _():
                arrived(k, 0)
                arrived(k, 1)

            @pl.when(jnp.logical_not(at_root))
            def _():
                arrived(k, mine)

                @pl.when(relays(k))
                def _():
                    ahead_send(k).start()

                pass_on(k).start()

    def share(u):
        return 8 if isinstance(u, int) and u >= GROUPS - 1 else 16

    def first_column(u):
        if isinstance(u, int) and u == GROUPS:
            return 32
        return row0(jnp.int32(u) if isinstance(u, int) else u)

    def panel_of(u):
        return 1 if isinstance(u, int) and u >= PER_PANEL else u // PER_PANEL

    def part(ref, u):
        return ref.at[u] if share(u) == 16 else ref.at[u, :, pl.ds(0, 8), :]

    def own(u, position):
        return pl.ds(pl.multiple_of(position * share(u), 8), share(u))

    def to_x(u):
        for d in range(1, NX):
            yield remote(
                wloc.at[u, own(u, lax.rem(x + d, NX)), :],
                x_land.at[u, d - 1, pl.ds(0, share(u)), :], x_s.at[u], x_r.at[u], x_peer(d),
            )

    def to_z(u):
        for d in range(1, NZ):
            ref = zs.at[u, pl.ds(0, share(u)), :]
            yield remote(ref, z_land.at[u, d - 1, pl.ds(0, share(u)), :], z_s.at[u], z_r.at[u], z_peer(d))

    def back_x(u):
        for d in range(1, NX):
            ref = red.at[u, pl.ds(0, share(u)), :]
            yield remote(ref, ag_land.at[u, d - 1, pl.ds(0, share(u)), :], ag_s.at[u], ag_r.at[u], x_peer(d))

    def whole(ref, send_sem, recv_sem):
        return remote(ref, ref, send_sem, recv_sem, ring(y, 1 - core))

    def project(u):
        count = share(u) * NX
        total = jnp.zeros((count, NB), F32)
        for h in range(2):
            high, low = split(vt[panel_of(u), h, pl.ds(first_column(u), count), :])
            both = dot(jnp.concatenate([high, low], axis=0), eh[h * HALF : (h + 1) * HALF, :])
            total += both[:count] + both[count:] + dot(high, el[h * HALF : (h + 1) * HALF, :])
        wloc[u, :count] = total
        for copy in to_x(u):
            copy.start()

    def sum_x(u):
        n = share(u)
        whole(part(x_land, u), x_s.at[u], x_r.at[u]).wait_recv()
        total = wloc[u, own(u, x), :]
        for d in range(NX - 1):
            total += x_land[u, d, :n]
        zs[u, :n] = total
        for copy in to_z(u):
            copy.start()

    def sum_z(u):
        n = share(u)
        whole(part(z_land, u), z_s.at[u], z_r.at[u]).wait_recv()
        total = zs[u, :n]
        for d in range(NZ - 1):
            total += z_land[u, d, :n]
        red[u, :n] = total
        for copy in back_x(u):
            copy.start()

    def gather(u):
        n = share(u)
        whole(part(ag_land, u), ag_s.at[u], ag_r.at[u]).wait_recv()
        base = panel_of(u) * NB + first_column(u)
        wfull[pl.ds(pl.multiple_of(base + x * n, 8), n), :] = red[u, :n]
        for d in range(1, NX):
            origin = lax.rem(x + NX - d, NX)
            wfull[pl.ds(pl.multiple_of(base + origin * n, 8), n), :] = ag_land[u, d - 1, :n]

    def transpose_first(j, h):
        columns = pl.ds(pl.multiple_of(j * TILE, TILE), TILE)
        for start in range(0, HALF, TILE):
            high, low = split(vt[0, h, columns, start : start + TILE].T)
            rows = pl.ds(pl.multiple_of(h * HALF + start, TILE), TILE)
            vn[0, rows, columns] = high
            vn[1, rows, columns] = low

    def transpose_upper(h):
        for start in range(0, HALF, TILE):
            high, low = split(vt[1, h, TILE:, start : start + TILE].T)
            rows = pl.ds(pl.multiple_of(h * HALF + start, TILE), TILE)
            vn[2, rows, :TILE] = high
            vn[2, rows, TILE:] = low

    def transpose_quarter(q):
        for start in range(0, ROWS, TILE):
            lanes = slice(start % HALF, start % HALF + TILE)
            high, low = split(vt[1, start // HALF, q * 64 : (q + 1) * 64, lanes])
            both = jnp.concatenate([high.astype(F32), low.astype(F32)], axis=0).T.astype(BF16)
            vn[3 + q, start : start + TILE, :TILE] = both
            vn[3 + q, start : start + TILE, TILE:] = both

    def m_to_z(m):
        for d in range(1, NZ):
            yield remote(ms.at[m], mz_land.at[m, d - 1], mz_s.at[m], mz_r.at[m], z_peer(d))

    def m_to_x(m):
        for d in range(1, NX):
            yield remote(mz.at[m], mx_land.at[m, d - 1], mx_s.at[m], mx_r.at[m], x_peer(d))

    def m_begin(m):
        is_source = at_root & ((core == 1) if m == 0 else (core == 0))

        @pl.when(jnp.logical_not(is_source | first))
        def _():
            whole(ms.at[m], ms_s.at[m], ms_r.at[m]).wait_recv()

        for copy in m_to_z(m):
            copy.start()

    def m_forward(m):
        whole(ms.at[m], ms_s.at[m], ms_r.at[m]).wait_recv()
        spread_on(m).start()

    def m_middle(m):
        whole(mz_land.at[m], mz_s.at[m], mz_r.at[m]).wait_recv()
        mz[m, pl.ds(pl.multiple_of(z * 8, 8), 8), :] = ms[m]
        for d in range(1, NZ):
            origin = lax.rem(z + NZ - d, NZ)
            mz[m, pl.ds(pl.multiple_of(origin * 8, 8), 8), :] = mz_land[m, d - 1]
        for copy in m_to_x(m):
            copy.start()

    def m_end(m):
        whole(mx_land.at[m], mx_s.at[m], mx_r.at[m]).wait_recv()
        mats[m, pl.ds(pl.multiple_of(x * 64, 64), 64), :] = mz[m]
        for d in range(1, NX):
            origin = lax.rem(x + NX - d, NX)
            mats[m, pl.ds(pl.multiple_of(origin * 64, 64), 64), :] = mx_land[m, d - 1]

    overlap_here = at_root & (core == 0)

    def overlap_to_z():
        for d in range(1, NZ):
            yield remote(gloc.at[lax.rem(z + d, NZ)], gz_land.at[d - 1], gz_s.at[0], gz_r.at[0], z_peer(d))

    def overlap_to_x():
        for d in range(1, NX):
            yield remote(gq.at[lax.rem(x + d, NX)], gx_land.at[d - 1], gx_s.at[0], gx_r.at[0], x_peer(d))

    def overlap_begin():
        total = jnp.zeros((NB, NB), F32)
        for h in range(2):
            ah, al = split(vt[1, h])
            bh, bl = split(vt[0, h])
            total += dot_nt(ah, bh) + dot_nt(ah, bl) + dot_nt(al, bh)
        gacc[...] = total
        for zz in range(NZ):
            for xx in range(NX):
                gloc[zz, xx] = gacc[xx * 64 + zz * 8 : xx * 64 + zz * 8 + 8, :]
        for copy in overlap_to_z():
            copy.start()

    def overlap_middle():
        whole(gz_land, gz_s.at[0], gz_r.at[0]).wait_recv()
        total = gloc[z]
        for d in range(NZ - 1):
            total += gz_land[d]
        gq[...] = total
        for copy in overlap_to_x():
            copy.start()

    def overlap_end():
        whole(gx_land, gx_s.at[0], gx_r.at[0]).wait_recv()
        total = gq[x]
        for d in range(NX - 1):
            total += gx_land[d]
        ms[2] = total
        for copy in spread(2):
            copy.start()

    def split_field():
        load_e.wait()

        def body(n, _):
            rows = pl.ds(pl.multiple_of(n * 256, 256), 256)
            high, low = split(e[rows, :])
            eh[rows, :] = high
            el[rows, :] = low
            return 0

        lax.fori_loop(0, ROWS // 256, body, 0)

    def when(condition, action, *args):
        pl.when(condition)(lambda: action(*args))

    def other_half(done, begin, end):
        @pl.when(jnp.logical_not(at_root))
        def _():
            for t in range(begin, end):
                arrived(done * TICKS + t, 1 - mine)

    def factors_end():
        m_end(0)
        m_end(1)

    def step(i, _):
        done = i - lag
        when(i < GROUPS, ticks, i, 0, 1)

        @pl.when(i == 0)
        def _():
            when(at_root, transpose_in, 1)

        @pl.when(i == 1)
        def _():
            hear(1)
            tell(2)

        @pl.when(done >= 0)
        def _():
            other_half(done, 0, TICKS)
            project(done)

        when(i < GROUPS, ticks, i, 1, 2)
        when(overlap_here & (i == 4), overlap_begin)
        when(overlap_here & (i == 6), overlap_middle)
        when(overlap_here & (i == 7), overlap_end)
        when(first & (i == 7), m_forward, 2)
        when(i == 7, m_begin, 2)
        when((done >= 1) & (i <= GROUPS), sum_x, done - 1)
        when((done >= 3) & (i <= GROUPS), sum_z, done - 3)
        when(i < GROUPS, ticks, i, 2, 3)

        @pl.when((i == GROUPS - 1) & last)
        def _():
            other_half(GROUPS - 1, 0, TICKS // 2)
            project(GROUPS - 1)

        when(i == 0, split_field)
        when((done >= 1) & (done <= 4), lambda: transpose_first((done - 1) // 2, (done - 1) % 2))
        when((done == 5) | (done == 6), lambda: transpose_upper(done - 5))
        when(i < GROUPS, ticks, i, 3, 4)

        @pl.when(i == 0)
        def _():
            hear(0)
            tell(1)

        @pl.when(i == 1)
        def _():
            hear(2)

            @pl.when(first)
            def _():
                m_forward(0)
                m_forward(1)


        @pl.when(done == 1)
        def _():
            m_begin(0)
            m_begin(1)

        @pl.when(done == 3)
        def _():
            m_middle(0)
            m_middle(1)

        when(done == 5, factors_end)
        return 0

    lax.fori_loop(0, GROUPS - 1 + lag, step, 0)

    def sums(action, begin, end):
        def body(u, _):
            action(u)
            return 0

        lax.fori_loop(begin, end, body, 0)

    caught_up = jnp.where(first, 1, 0)
    sums(sum_x, GROUPS - 1 - lag + caught_up, GROUPS - 2)

    @pl.when(jnp.logical_not(last))
    def _():
        other_half(GROUPS - 1, 0, TICKS // 2)
        project(GROUPS - 1)

    other_half(GROUPS - 1, TICKS // 2, TICKS)
    project(GROUPS)

    def left(u):
        whole(part(x_land, u), x_s.at[u], x_r.at[u]).wait_send()
        whole(part(z_land, u), z_s.at[u], z_r.at[u]).wait_send()
        whole(part(ag_land, u), ag_s.at[u], ag_r.at[u]).wait_send()

    def matrices_left():
        for m in range(3):
            whole(mz_land.at[m], mz_s.at[m], mz_r.at[m]).wait_send()
            whole(mx_land.at[m], mx_s.at[m], mx_r.at[m]).wait_send()

            @pl.when(at_root & ((core == 1) if m == 0 else (core == 0)))
            def _():
                whole(mz_land.at[m, pl.ds(0, 5)], ms_s.at[m], ms_r.at[m]).wait_send()

            @pl.when(first)
            def _():
                spread_on(m).wait_send()

        @pl.when(overlap_here)
        def _():
            whole(gz_land, gz_s.at[0], gz_r.at[0]).wait_send()
            whole(gx_land, gx_s.at[0], gx_r.at[0]).wait_send()

    def stream_left():
        @pl.when(jnp.logical_not(at_root))
        def _():
            whole(vt.at[:, mine], sib.at[0], sib.at[0]).wait_send()

            @pl.when(jnp.logical_not(last))
            def _():
                whole(vt.at[0, mine], passed.at[0], sib.at[0]).wait_send()

            @pl.when(first)
            def _():
                whole(vt.at[1, mine], passed.at[1], sib.at[0]).wait_send()

            @pl.when(y == 2)
            def _():
                sent = NB - (CHUNKS - DIRECT) * TICK
                whole(vt.at[1, mine, pl.ds(0, sent), :], passed.at[1], sib.at[0]).wait_send()

        @pl.when(at_root)
        def _():
            whole(vt.at[1 - core], sib.at[0], sib.at[0]).wait_send()
            base = (1 - core) * (CHUNKS // 2)
            for h in range(2):
                for t in range(CHUNKS // 2 - DEPTH, CHUNKS // 2):
                    ring_send(base + t, h).wait_send()

        @pl.when(at_root & (core == 0))
        def _():
            for h in range(2):
                for k in range(DIRECT, CHUNKS):
                    direct_send(k, h).wait_send()

    def quarter(q, value):
        high, low = split(value)
        stacked = jnp.concatenate([high, high, low, jnp.zeros_like(low)], axis=0)
        return dot(vn[3 + q], stacked)

    sums(sum_z, GROUPS - 3 - lag + caught_up, GROUPS - 4)
    sum_x(6)
    sum_z(4)
    m_middle(2)
    for u in range(4):
        gather(u)
    first_s = product(mats[0], wfull[:NB, :])
    high, low = split(first_s)
    e[...] -= dot(vn[0], high) + dot(vn[0], low) + dot(vn[1], high)
    sum_x(7)
    transpose_quarter(1)
    sum_x(8)
    transpose_quarter(0)
    sum_z(5)
    stream_left()
    gather(4)
    m_end(2)
    correction = product(mats[2], first_s)
    sum_z(6)
    gather(5)
    upper = wfull[NB + TILE :, :] - correction[TILE:]
    high, low = split(product(mats[1, TILE:, TILE:], upper))
    sum_z(7)
    sum_z(8)
    matrices_left()
    e[...] -= dot(vn[2], jnp.concatenate([high, high], axis=0)) + dot(vn[2, :, :TILE], low)
    gather(6)
    next_u = wfull[NB + 64 : NB + TILE, :] - correction[64:TILE]
    known_u = jnp.concatenate([jnp.zeros_like(next_u), next_u, upper], axis=0)
    e[...] -= quarter(1, product(mats[1, 64:TILE, :], known_u))
    gather(7)
    gather(8)
    for u in range(UNITS):
        left(u)
    last_u = wfull[NB : NB + 64, :] - correction[:64]
    out[...] = e[...] - quarter(0, product(mats[1, :64, :], jnp.concatenate([last_u, next_u, upper], axis=0)))


def local(eigvecs, reflectors, factors):
    vmem, dma = pltpu.VMEM, pltpu.SemaphoreType.DMA
    return pl.pallas_call(
        kernel,
        out_shape=jax.ShapeDtypeStruct((ROWS, NB), F32),
        in_specs=[pl.BlockSpec(memory_space=pltpu.HBM)] * 3,
        out_specs=pl.BlockSpec(memory_space=pltpu.VMEM),
        scratch_shapes=[
            vmem((ROWS, NB), F32),
            vmem((ROWS, NB), F32),
            vmem((ROWS, NB), BF16),
            vmem((ROWS, NB), BF16),
            vmem((2, 2, NB, HALF), F32),
            vmem((5, ROWS, NB), BF16),
            vmem((UNITS, GROUP, NB), F32),
            vmem((UNITS, NX - 1, 16, NB), F32),
            vmem((UNITS, 16, NB), F32),
            vmem((UNITS, NZ - 1, 16, NB), F32),
            vmem((UNITS, 16, NB), F32),
            vmem((UNITS, NX - 1, 16, NB), F32),
            vmem((2 * NB, NB), F32),
            vmem((3, 8, NB), F32),
            vmem((3, NZ - 1, 8, NB), F32),
            vmem((3, 64, NB), F32),
            vmem((3, NX - 1, 64, NB), F32),
            vmem((3, NB, NB), F32),
            vmem((NB, NB), F32),
            vmem((NZ, NX, 8, NB), F32),
            vmem((NZ - 1, NX, 8, NB), F32),
            vmem((NX, 8, NB), F32),
            vmem((NX - 1, 8, NB), F32),
            pltpu.SemaphoreType.REGULAR((3, 3)),
            dma((3,)),
            dma((2, CHUNKS)),
            dma((2, CHUNKS)),
            dma((1,)),
            dma((2,)),
            dma((2, CHUNKS - DIRECT)),
            *[dma((UNITS,))] * 6,
            *[dma((3,))] * 6,
            *[dma((1,))] * 4,
        ],
        compiler_params=pltpu.CompilerParams(collective_id=0, has_side_effects=True, vmem_limit_bytes=50 * 2**20),
    )(eigvecs, reflectors, factors)


def solution(mesh):
    in_specs = (P("row", "col"), P("row", "col"), P("col", None, None))
    return jax.shard_map(local, mesh=mesh, in_specs=in_specs, out_specs=P("row", "col"), check_vma=False)
```
